32 devices in a mesh: groups: 2 (over y), expert: 4 (over z), sub: 2 (over x), pair: 2 (over core).
Axes of the slice: x: 2, y: 2, z: 4, core: 2. Of those that a mesh axis runs over, the one named last changes fastest.
Arguments:
- tokens: bfloat16 [4096, 2048], P(('groups', 'expert', 'sub', 'pair')), parts along dimension 0, may hold values from -6 to 6
- out_grad: bfloat16 [4096, 2048], P(('groups', 'expert', 'sub', 'pair')), parts along dimension 0, may hold values from -6 to 6
- routes: int32 [4096, 8], P(('groups', 'expert', 'sub', 'pair')), parts along dimension 0, may hold values from 0 to 127, as said below
- route_weight: bfloat16 [4096, 8], P(('groups', 'expert', 'sub', 'pair')), parts along dimension 0, may hold values from 0.099609375 to 1
- example_id: int32 [4096], P(('groups', 'expert', 'sub', 'pair')), parts along dimension 0, may hold values from 0 to 15, never falling along the last dimension, each value on 1 to 512 neighbouring positions
- gate_w: bfloat16 [4, 2048, 1024], P('expert', 'sub', 'pair'), may hold values from -0.125 to 0.125
- up_w: bfloat16 [4, 2048, 1024], P('expert', 'sub', 'pair'), may hold values from -0.125 to 0.125
- down_w: bfloat16 [4, 1024, 2048], P('expert', 'pair', 'sub'), may hold values from -0.1875 to 0.1875
- proj_grad: bfloat16 [64, 2048], replicated, may hold values from -0.125 to 0.125
- proj_hidden: bfloat16 [64, 1024], P(None, 'pair'), may hold values from -0.1875 to 0.1875
Outputs:
- input_grad: bfloat16 [4096, 2048], P(('groups', 'expert', 'sub', 'pair')), parts along dimension 0
- example_grads: float32 [32, 4, 64, 64], P(('groups', 'expert'), None, ('sub', 'pair')), parts along dimension 0
The draws below stay inside these ranges and needn't reach their ends.
There are 2 independent parts, one for each index of `groups`. The reference program is written for one: setup_inputs(seed, part) draws one part's arguments, and reference() takes and returns one part's arrays. A program takes and returns all parts, laid end to end along the dimension named above; an argument that names none is the same for every part. Nothing has to cross between parts.
Inputs may be any that keep to these rules, and one draw needn't show every extreme that they name: `routes`: each row names 8 different experts. Within the rows of one device (aligned blocks of 128 rows) no expert below 4 is named by more than 10 rows, and one such expert is named by exactly 10 rows in every block.
All inputs are finite; a program needn't handle non-finite values.
Results may differ from the reference program's by a relative error of at most 0.01.
Values may be sent and summed in bfloat16 or wider, within the bound.
A program may use at most 128 MiB of HBM per device.

```python
import math
import jax
import jax.numpy as jnp
import numpy as np
from jax import lax

D = 2048
FF = 1024
EXPERTS = 128
TOP = 8
RANK = 64
TOK_DEV = 128
CAP = 10
WIN = 4
EXAMPLES = 16
TOKENS = 2048
MOST_LEN = 512
N_PAIR = 2


def draw_routes(key, part):
    key = jax.random.fold_in(key, 7)
    first, second, third = jax.random.split(key, 3)
    level = jax.random.randint(first, (EXPERTS,), 0, 4)
    favoured = jax.random.randint(second, (), 0, WIN)
    noise = jax.random.randint(third, (TOKENS // TOK_DEV, TOK_DEV, EXPERTS), 0, 1024)
    labels = jnp.arange(EXPERTS, dtype=jnp.int32)
    scores = (noise + level[None, None, :] * 256) * EXPERTS + labels[None, None, :]
    scores = scores + jnp.where(labels == favoured, 1 << 24, 0)[None, None, :]

    def one_block(block_scores):

        def step(counts, row):
            full = (counts >= CAP) & (labels < WIN)
            masked = jnp.where(full, -1 - labels, row)
            values, picked = lax.top_k(masked, TOP)
            counts = counts + jnp.sum((picked[:, None] == labels[None, :]).astype(jnp.int32), axis=0)
            return (counts, picked)
        final, picks = lax.scan(step, jnp.zeros((EXPERTS,), jnp.int32), block_scores)
        return picks
    picks = jax.vmap(one_block)(scores)
    return picks.reshape(TOKENS, TOP).astype(jnp.int32)


def levels(own_key, extent, cuts, low, high):
    def one(axis_at, blocks):
        heights = jax.random.uniform(jax.random.fold_in(jax.random.fold_in(own_key, 6), axis_at), (blocks,), jnp.float32, low / len(cuts), high / len(cuts))
        return jnp.repeat(jnp.exp(heights), extent[axis_at] // blocks).reshape((-1,) + (1,) * (len(extent) - axis_at - 1))

    loudness = one(*cuts[0])
    for cut in cuts[1:]:
        loudness = loudness * one(*cut)
    return loudness


def length_profile(amount, total, bound, skew):
    weights = [(1 << 20) // math.isqrt(grade ** skew) + 1 for grade in range(2, amount + 1)]
    rest, given = total - bound - (amount - 1), [1] * (amount - 1)
    while rest > 0:
        free = [i for i in range(amount - 1) if given[i] < bound]
        mass, budget = sum([weights[i] for i in free]), rest
        for i in free:
            more = min(bound - given[i], max(1, budget * weights[i] // mass), rest)
            given[i] = given[i] + more
            rest = rest - more
    return np.array([bound] + given)


def ragged_sizes(key, number_of, total, most, slope):
    if number_of == 2:
        one = jax.random.randint(key, (), max(1, total - most), min(most, total - 1) + 1)
        return jnp.stack([one, total - one])
    tallies = jnp.asarray(length_profile(number_of, total, most, slope), jnp.int32)
    twos = (number_of - 1) // 2
    source_of, taker = tallies[1:1 + 2 * twos:2], tallies[2:2 + 2 * twos:2]
    margin = jnp.minimum(source_of - 1, most - taker)
    moved = jax.random.randint(jax.random.fold_in(key, 1), (twos,), 0, 1 << 20) % (margin + 1)
    tallies = tallies.at[1:1 + 2 * twos:2].set(source_of - moved).at[2:2 + 2 * twos:2].set(taker + moved)
    return tallies[jax.random.permutation(jax.random.fold_in(key, 2), number_of)]


def centred(own_key, extent, spread, reach, cuts=(), kind=jnp.bfloat16):
    entries = jax.random.normal(own_key, extent, jnp.float32) * spread
    if len(cuts) > 0:
        entries = levels(own_key, extent, cuts, -0.22, 0.18) * entries
    return jnp.clip(entries, min=-reach, max=reach).astype(kind)


def setup_inputs(seed: int = 0, part: int = 0) -> dict:
    keys = jax.random.split(jax.random.key(seed), 11)
    own_keys = jax.random.split(jax.random.fold_in(keys[10], part), 11)
    return {
        "tokens": centred(own_keys[0], (TOKENS, D), 1.0, 6.0, ((0, 16),)),
        "out_grad": centred(own_keys[1], (TOKENS, D), 1.0, 6.0, ((0, 16),)),
        "routes": draw_routes(jax.random.fold_in(jax.random.fold_in(keys[10], part), 71), part),
        "route_weight": jnp.clip(jnp.exp(math.log(1.0) - 2.306499 * jax.random.uniform(own_keys[3], (TOKENS, TOP), jnp.float32) ** levels(own_keys[3], (TOKENS, TOP), ((0, 16),), -0.2, 0.2)), 0.099609375, 1.0).astype(jnp.bfloat16),
        "example_id": jnp.searchsorted(jnp.cumsum(ragged_sizes(own_keys[4], EXAMPLES, TOKENS, MOST_LEN, 1)), jnp.arange(TOKENS), side="right").astype(jnp.int32),
        "gate_w": centred(keys[5], (WIN, D, FF), D ** -0.5, 0.125, ((0, 4), (1, 2), (2, 2))),
        "up_w": centred(keys[6], (WIN, D, FF), D ** -0.5, 0.125, ((0, 4), (1, 2), (2, 2))),
        "down_w": centred(keys[7], (WIN, FF, D), FF ** -0.5, 0.1875, ((0, 4), (1, 2), (2, 2))),
        "proj_grad": centred(keys[8], (RANK, D), D ** -0.5, 0.125),
        "proj_hidden": centred(keys[9], (RANK, FF), FF ** -0.5, 0.1875, ((1, 2),)),
    }


def reference(tokens, out_grad, routes, route_weight, example_id, gate_w, up_w, down_w, proj_grad, proj_hidden):
    halves = N_PAIR
    blocks = TOKENS // TOK_DEV
    per_block = TOK_DEV * TOP
    route_flat = routes.reshape(blocks, per_block)
    inside = route_flat < WIN
    owner_hot = ((route_flat[:, :, None] == jnp.arange(WIN, dtype=jnp.int32)[None, None, :]) & inside[:, :, None]).astype(jnp.int32)
    earlier = jnp.cumsum(owner_hot, axis=1) - owner_hot
    position = jnp.sum(earlier * owner_hot, axis=2)
    weight_flat = route_weight.reshape(blocks, per_block)
    slice_width = FF // halves

    def one_expert(total, inputs):
        gate_e, up_e, down_e, expert = inputs
        match = ((route_flat == expert)[:, :, None] & (position[:, :, None] == jnp.arange(CAP, dtype=jnp.int32)[None, None, :])).astype(jnp.int32)
        valid = jnp.sum(match, axis=1).reshape(-1) > 0
        index = jnp.sum(match * jnp.arange(per_block, dtype=jnp.int32)[None, :, None], axis=1)
        token_index = (jnp.arange(blocks, dtype=jnp.int32)[:, None] * TOK_DEV + index // TOP).reshape(-1).astype(jnp.int32)
        weight_row = jnp.take_along_axis(weight_flat, index, axis=1).reshape(-1)
        rows_x = jnp.where(valid[:, None], tokens[token_index], jnp.zeros((), jnp.bfloat16))
        scaled = (weight_row.astype(jnp.float32)[:, None] * out_grad[token_index].astype(jnp.float32))
        scaled = jnp.where(valid[:, None], scaled, jnp.float32(0.0)).astype(jnp.bfloat16)
        codes = jnp.where(valid, example_id[token_index], -1)
        gate_pre = jnp.dot(rows_x, gate_e, preferred_element_type=jnp.float32)
        up_pre = jnp.dot(rows_x, up_e, preferred_element_type=jnp.float32)
        sigmoid_gate = jax.nn.sigmoid(gate_pre)
        silu_gate = gate_pre * sigmoid_gate
        hidden = (silu_gate * up_pre).astype(jnp.bfloat16)
        hidden_grad = jnp.dot(scaled, down_e.T, preferred_element_type=jnp.float32)
        gate_grad = (hidden_grad * up_pre * sigmoid_gate * (1.0 + gate_pre * (1.0 - sigmoid_gate))).astype(jnp.bfloat16)
        up_grad = (hidden_grad * silu_gate).astype(jnp.bfloat16)
        rows_count = gate_grad.shape[0]
        gate_parts = jnp.einsum("rgf,dgf->grd", gate_grad.astype(jnp.float32).reshape(rows_count, halves, slice_width), gate_e.astype(jnp.float32).reshape(D, halves, slice_width))
        up_parts = jnp.einsum("rgf,dgf->grd", up_grad.astype(jnp.float32).reshape(rows_count, halves, slice_width), up_e.astype(jnp.float32).reshape(D, halves, slice_width))
        parts = (gate_parts + up_parts).astype(jnp.bfloat16).astype(jnp.float32)
        route_grad = jnp.sum(parts, axis=0).astype(jnp.bfloat16)
        total = total.at[token_index].add(route_grad.astype(jnp.float32))
        grad_proj = jnp.dot(scaled, proj_grad.T, preferred_element_type=jnp.float32).astype(jnp.bfloat16)
        hidden_proj = jnp.dot(hidden, proj_hidden.T, preferred_element_type=jnp.float32)
        example_hot = (codes[:, None] == jnp.arange(EXAMPLES, dtype=jnp.int32)[None, :]).astype(jnp.float32)
        block = jnp.einsum("re,ra,rb->eab", example_hot, grad_proj.astype(jnp.float32), hidden_proj, precision=lax.Precision.HIGHEST)
        return total, block

    start = jnp.zeros((TOKENS, D), jnp.float32)
    total, stacked = lax.scan(one_expert, start, (gate_w, up_w, down_w, jnp.arange(WIN, dtype=jnp.int32)))
    return total.astype(jnp.bfloat16), jnp.transpose(stacked, (1, 0, 2, 3))
```

```python
import functools

import jax
import jax.numpy as jnp
from jax import lax
from jax.experimental import pallas as pl
from jax.experimental.pallas import tpu as pltpu
from jax.sharding import PartitionSpec as P

CAP = 10
PAD = 16
GROUP = 8
BLOCK = CAP * GROUP
LANES = 128
MESH = pl.DeviceIdType.MESH
F32 = jnp.float32
BF16 = jnp.bfloat16
NT = (((1,), (1,)), ((), ()))
TN = (((0,), (0,)), ((), ()))


def dot(a, b, dims=(((1,), (0,)), ((), ()))):
    return lax.dot_general(a, b, dims, preferred_element_type=F32)


def pack_matrix(rows, cols):
    i = lax.broadcasted_iota(jnp.int32, (rows, cols), 0)
    k = lax.broadcasted_iota(jnp.int32, (rows, cols), 1)
    hit = (k // PAD == i // CAP) & (k % PAD == i % CAP)
    return jnp.where(hit, 1.0, 0.0).astype(BF16)


def kernel(
    owners, subs, rank_size,
    payload, pick, gate, up, down, ph,
    out, eg_out,
    buf, comp, rs_send, rs_own, rs_buf, gbuf, hp_buf, rp, rp_in, ret_send, ret_buf, gs, eg_buf,
    d_send, d_recv, f_send, f_recv, rs_ss, rs_rs, g_ss, g_rs, h_ss, h_rs, p_ss, p_rs,
    r_ss, r_rs, e_ss, e_rs, l_sem,
):
    ei, si, pi = lax.axis_index("expert"), lax.axis_index("sub"), lax.axis_index("pair")
    other = 1 - pi
    sources = owners * subs
    me = ei * subs + si
    rows = comp.shape[0]
    half = rows // 2
    chunk = rows // subs
    wide = payload.shape[1] // subs
    dh = (wide - LANES) // 2
    ff = gate.shape[1]

    barrier = pltpu.get_barrier_semaphore()

    def greet(d, c):
        j = lax.rem(me + d, sources)
        pl.semaphore_signal(
            barrier, 1, device_id={"expert": j // subs, "sub": j % subs}, device_id_type=MESH
        )
        return c

    lax.fori_loop(1, sources, greet, 0)
    for d in range(subs):
        pl.semaphore_signal(
            barrier, 1, device_id={"sub": lax.rem(si + d, subs), "pair": other}, device_id_type=MESH
        )
    pl.semaphore_wait(barrier, sources - 1 + subs)

    def padded(j):
        return pl.ds(pl.multiple_of(j * PAD, PAD), PAD)

    def dispatch(d):
        j = lax.rem(me + d, sources)
        e, s = j // subs, j % subs
        return pltpu.make_async_remote_copy(
            src_ref=payload.at[padded(e), pl.ds(pl.multiple_of(s * wide, LANES), wide)],
            dst_ref=buf.at[pi, padded(me)],
            send_sem=d_send.at[j],
            recv_sem=d_recv.at[me],
            device_id={"expert": e, "sub": s},
            device_id_type=MESH,
        )

    def start_dispatch(d, c):
        dispatch(d).start()
        return c

    lax.fori_loop(1, sources, start_dispatch, 0)
    mine = payload.at[padded(ei), pl.ds(pl.multiple_of(si * wide, LANES), wide)]
    local = pltpu.make_async_copy(mine, buf.at[pi, padded(me)], l_sem)
    local.start()

    def arrived(j):
        return pltpu.make_async_remote_copy(
            src_ref=buf.at[pi, padded(j)],
            dst_ref=buf.at[pi, padded(j)],
            send_sem=d_send.at[j],
            recv_sem=d_recv.at[j],
            device_id={"expert": j // subs, "sub": j % subs},
            device_id_type=MESH,
        )

    def forward(j, half_at):
        return pltpu.make_async_remote_copy(
            src_ref=buf.at[half_at, padded(j)],
            dst_ref=buf.at[half_at, padded(j)],
            send_sem=f_send.at[j],
            recv_sem=f_recv.at[j],
            device_id={"pair": other},
            device_id_type=MESH,
        )

    local.wait()
    forward(me, pi).start()

    def pass_on(d, c):
        j = lax.rem(me - d + sources, sources)
        arrived(j).wait_recv()
        forward(j, pi).start()
        return c

    lax.fori_loop(1, sources, pass_on, 0)

    squeeze = pack_matrix(BLOCK, GROUP * PAD)

    def compact(half_at):
        def body(g, c):
            part = buf[half_at, pl.ds(pl.multiple_of(g * GROUP * PAD, GROUP * PAD), GROUP * PAD), :]
            at = pl.multiple_of(half_at * half + g * BLOCK, PAD)
            comp[pl.ds(at, BLOCK), :] = dot(squeeze, part).astype(BF16)
            return c

        lax.fori_loop(0, sources // GROUP, body, 0)

    compact(pi)

    def take_pass(j, c):
        forward(j, other).wait_recv()
        return c

    lax.fori_loop(0, sources, take_pass, 0)
    compact(other)

    def partial(at, store):
        x = comp[pl.ds(at, BLOCK), 0:dh]
        z = comp[pl.ds(at, BLOCK), dh : 2 * dh]
        store(0, dot(x, gate[...]))
        store(1, dot(x, up[...]))
        store(2, dot(z, down[...], NT))

    def rs_copy(d):
        s = lax.rem(si + d, subs)
        return pltpu.make_async_remote_copy(
            src_ref=rs_send.at[pl.ds(pl.multiple_of(s * chunk, PAD), chunk)],
            dst_ref=rs_buf.at[si],
            send_sem=rs_ss.at[s],
            recv_sem=rs_rs.at[si],
            device_id={"sub": s},
            device_id_type=MESH,
        )

    for d in range(1, subs):
        base = lax.rem(si + d, subs) * chunk

        def send_block(b, c):
            at = pl.multiple_of(base + b * BLOCK, PAD)

            def store(k, v):
                rs_send[pl.ds(at, BLOCK), k * ff : (k + 1) * ff] = v.astype(BF16)

            partial(at, store)
            return c

        lax.fori_loop(0, chunk // BLOCK, send_block, 0)
        rs_copy(d).start()

    def own_block(b, c):
        to = pl.multiple_of(b * BLOCK, PAD)

        def store(k, v):
            rs_own[pl.ds(to, BLOCK), k * ff : (k + 1) * ff] = v

        partial(pl.multiple_of(si * chunk + b * BLOCK, PAD), store)
        return c

    lax.fori_loop(0, chunk // BLOCK, own_block, 0)

    def rs_wait(d):
        s = lax.rem(si + d, subs)
        return pltpu.make_async_remote_copy(
            src_ref=rs_buf.at[s],
            dst_ref=rs_buf.at[s],
            send_sem=rs_ss.at[s],
            recv_sem=rs_rs.at[s],
            device_id={"sub": s},
            device_id_type=MESH,
        )

    for d in range(1, subs):
        rs_wait(d).wait_recv()

    hp_me = si * 2 + pi

    def act_block(b, c):
        to = pl.multiple_of(b * BLOCK, PAD)

        def total(k):
            v = rs_own[pl.ds(to, BLOCK), k * ff : (k + 1) * ff]
            for d in range(1, subs):
                s = lax.rem(si + d, subs)
                v = v + rs_buf[s, pl.ds(to, BLOCK), k * ff : (k + 1) * ff].astype(F32)
            return v

        g, u, h = total(0), total(1), total(2)
        sig = 1.0 / (1.0 + jnp.exp(-g))
        silu = g * sig
        at = pl.multiple_of(si * chunk + b * BLOCK, PAD)
        gbuf[pl.ds(at, BLOCK), 0:ff] = (h * u * sig * (1.0 + g * (1.0 - sig))).astype(BF16)
        gbuf[pl.ds(at, BLOCK), ff : 2 * ff] = (h * silu).astype(BF16)
        hp_buf[hp_me, pl.ds(to, BLOCK), :] = dot((silu * u).astype(BF16), ph[...], NT)
        return c

    lax.fori_loop(0, chunk // BLOCK, act_block, 0)

    def g_copy(d, came):
        s = lax.rem(si + d, subs)
        at = s if came else si
        span = gbuf.at[pl.ds(pl.multiple_of(at * chunk, PAD), chunk)]
        return pltpu.make_async_remote_copy(
            src_ref=span,
            dst_ref=span,
            send_sem=g_ss.at[s],
            recv_sem=g_rs.at[at],
            device_id={"sub": s},
            device_id_type=MESH,
        )

    def h_copy(d, came):
        q = lax.rem(hp_me + d, 2 * subs)
        at = q if came else hp_me
        return pltpu.make_async_remote_copy(
            src_ref=hp_buf.at[at],
            dst_ref=hp_buf.at[at],
            send_sem=h_ss.at[q],
            recv_sem=h_rs.at[at],
            device_id={"sub": q // 2, "pair": q % 2},
            device_id_type=MESH,
        )

    for d in range(1, subs):
        g_copy(d, False).start()
    for d in range(1, 2 * subs):
        h_copy(d, False).start()

    def route_chunk(s):
        def body(b, c):
            at = pl.multiple_of(s * chunk + b * BLOCK, PAD)
            v = dot(gbuf[pl.ds(at, BLOCK), 0:ff], gate[...], NT)
            v = v + dot(gbuf[pl.ds(at, BLOCK), ff : 2 * ff], up[...], NT)
            rp[pl.ds(at, BLOCK), :] = v.astype(BF16)
            return c

        lax.fori_loop(0, chunk // BLOCK, body, 0)

    route_chunk(si)
    for d in range(1, subs):
        g_copy(d, True).wait_recv()
        route_chunk(lax.rem(si + d, subs))

    swap = pltpu.make_async_remote_copy(
        src_ref=rp.at[pl.ds(pl.multiple_of(other * half, PAD), half)],
        dst_ref=rp_in,
        send_sem=p_ss,
        recv_sem=p_rs,
        device_id={"pair": other},
        device_id_type=MESH,
    )
    swap.start()
    swap.wait_recv()

    def sum_block(g, c):
        to = pl.multiple_of(g * BLOCK, PAD)
        at = pl.multiple_of(pi * half + g * BLOCK, PAD)
        v = rp[pl.ds(at, BLOCK), :].astype(F32) + rp_in[pl.ds(to, BLOCK), :].astype(F32)
        put = pl.multiple_of(g * GROUP * PAD, GROUP * PAD)
        ret_send[pl.ds(put, GROUP * PAD), :] = dot(squeeze, v.astype(BF16), TN).astype(BF16)
        return c

    lax.fori_loop(0, sources // GROUP, sum_block, 0)

    def back(j, came):
        at_e = j // subs if came else ei
        at_s = j % subs if came else si
        return pltpu.make_async_remote_copy(
            src_ref=ret_send.at[padded(j)],
            dst_ref=ret_buf.at[padded(at_e), pl.ds(pl.multiple_of(at_s * dh, LANES), dh)],
            send_sem=r_ss.at[j],
            recv_sem=r_rs.at[j if came else me],
            device_id={"expert": j // subs, "sub": j % subs},
            device_id_type=MESH,
        )

    def start_back(d, c):
        back(lax.rem(me + d, sources), False).start()
        return c

    lax.fori_loop(1, sources, start_back, 0)
    ret_buf[padded(ei), pl.ds(pl.multiple_of(si * dh, LANES), dh)] = ret_send[padded(me), :]

    for d in range(1, 2 * subs):
        h_copy(d, True).wait_recv()
    share = rank_size // (2 * subs)
    spread_cols = gs.shape[0]
    row = lax.broadcasted_iota(jnp.int32, (LANES, spread_cols), 0)
    col = lax.broadcasted_iota(jnp.int32, (LANES, spread_cols), 1)
    repeat = jnp.where(row == hp_me * share + col % share, 1.0, 0.0).astype(BF16)
    code_row = jnp.where(row == rank_size, 1.0, 0.0).astype(BF16)
    want = (
        lax.broadcasted_iota(jnp.int32, (BLOCK, spread_cols), 1) // share + 1
    ).astype(F32)

    def example_block(b, acc):
        at = pl.multiple_of(b * BLOCK, PAD)
        extra = comp[pl.ds(at, BLOCK), 2 * dh : wide]
        spread = jnp.where(dot(extra, code_row) == want, dot(extra, repeat), 0.0).astype(BF16)
        s = b // (chunk // BLOCK)
        to = pl.multiple_of((b % (chunk // BLOCK)) * BLOCK, PAD)
        hp = hp_buf[2 * s, pl.ds(to, BLOCK), :] + hp_buf[2 * s + 1, pl.ds(to, BLOCK), :]
        hi = hp.astype(BF16)
        rest = hp - hi.astype(F32)
        mid = rest.astype(BF16)
        low = (rest - mid.astype(F32)).astype(BF16)
        return acc + dot(spread, hi, TN) + dot(spread, mid, TN) + dot(spread, low, TN)

    gs[...] = lax.fori_loop(
        0, rows // BLOCK, example_block, jnp.zeros((spread_cols, LANES), F32)
    ).astype(BF16)
    piece = spread_cols // owners

    def e_copy(e, came):
        return pltpu.make_async_remote_copy(
            src_ref=gs.at[pl.ds(pl.multiple_of(e * piece, PAD), piece)],
            dst_ref=eg_buf.at[e if came else ei],
            send_sem=e_ss.at[e],
            recv_sem=e_rs.at[e if came else ei],
            device_id={"expert": e},
            device_id_type=MESH,
        )

    def start_e(d, c):
        e_copy(lax.rem(ei + d, owners), False).start()
        return c

    lax.fori_loop(1, owners, start_e, 0)
    eg_buf[ei] = gs[pl.ds(pl.multiple_of(ei * piece, PAD), piece), :]

    def take_back(d, c):
        back(lax.rem(me + d, sources), True).wait_recv()
        return c

    lax.fori_loop(1, sources, take_back, 0)
    out[...] = dot(pick[...], ret_buf[...], TN).astype(BF16)

    def take_e(d, c):
        e_copy(lax.rem(ei + d, owners), True).wait_recv()
        return c

    lax.fori_loop(1, owners, take_e, 0)
    eg_out[...] = eg_buf[...].astype(F32)

    def sent(d, c):
        j = lax.rem(me + d, sources)
        dispatch(d).wait_send()
        back(j, False).wait_send()
        return c

    lax.fori_loop(1, sources, sent, 0)

    def sent_pass(j, c):
        forward(j, pi).wait_send()
        return c

    lax.fori_loop(0, sources, sent_pass, 0)
    for d in range(1, subs):
        rs_copy(d).wait_send()
        g_copy(d, False).wait_send()
    for d in range(1, 2 * subs):
        h_copy(d, False).wait_send()
    swap.wait_send()

    def sent_e(d, c):
        e_copy(lax.rem(ei + d, owners), False).wait_send()
        return c

    lax.fori_loop(1, owners, sent_e, 0)


def per_device(
    tokens, out_grad, routes, route_weight, example_id, gate_w, up_w, down_w, proj_grad, proj_hidden
):
    owners = lax.axis_size("expert")
    subs = lax.axis_size("sub")
    local_tokens, width = tokens.shape
    fanout = routes.shape[1]
    rank_size = proj_grad.shape[0]
    slots = owners * PAD
    dh = width // subs
    wide = 2 * dh + LANES
    ff = gate_w.shape[2]
    sources = owners * subs
    rows = sources * 2 * CAP
    chunk = rows // subs
    examples = 4 * owners
    share = rank_size // (2 * subs)
    route_flat = routes.reshape(-1)
    inside = route_flat < owners
    named = (
        routes[:, :, None] == jnp.arange(owners, dtype=jnp.int32)[None, None, :]
    )
    taken = jnp.any(named, axis=1)
    order = (
        jnp.arange(local_tokens)[:, None] > jnp.arange(local_tokens)[None, :]
    ).astype(BF16)
    before = dot(order, taken.astype(BF16)).astype(jnp.int32)
    weight = jnp.sum(
        jnp.where(named, route_weight.astype(F32)[:, :, None], 0.0), axis=1
    )
    hit = (
        before.T[:, None, :] == jnp.arange(PAD, dtype=jnp.int32)[None, :, None]
    ) & taken.T[:, None, :]
    pick_token = hit.astype(BF16).reshape(slots, local_tokens)
    slot_weight = jnp.sum(jnp.where(hit, weight.T[:, None, :], 0.0), axis=2).reshape(slots)
    slot_code = jnp.sum(
        jnp.where(hit, (example_id + 1).astype(F32)[None, None, :], 0.0), axis=2
    ).reshape(slots)
    rows_in = dot(pick_token, tokens).astype(BF16)
    rows_grad = (slot_weight[:, None] * dot(pick_token, out_grad)).astype(BF16)
    slot_proj = dot(rows_grad, proj_grad, NT).astype(BF16)
    extra = jnp.concatenate(
        [
            slot_proj,
            slot_code.astype(BF16)[:, None],
            jnp.zeros((slots, LANES - rank_size - 1), BF16),
        ],
        axis=1,
    )
    parts = []
    for s in range(subs):
        parts += [rows_in[:, s * dh : (s + 1) * dh], rows_grad[:, s * dh : (s + 1) * dh], extra]
    payload = jnp.concatenate(parts, axis=1)
    ph = jnp.concatenate(
        [proj_hidden, jnp.zeros((LANES - rank_size, proj_hidden.shape[1]), BF16)], axis=0
    )
    vmem = pl.BlockSpec(memory_space=pltpu.VMEM)
    dma = pltpu.SemaphoreType.DMA
    piece = 4 * share
    input_grad, eg = pl.pallas_call(
        functools.partial(kernel, owners, subs, rank_size),
        out_shape=(
            jax.ShapeDtypeStruct((local_tokens, width), BF16),
            jax.ShapeDtypeStruct((owners, piece, LANES), F32),
        ),
        in_specs=[vmem] * 6,
        out_specs=(vmem, vmem),
        scratch_shapes=[
            pltpu.VMEM((2, sources * PAD, wide), BF16),
            pltpu.VMEM((rows, wide), BF16),
            pltpu.VMEM((rows, 3 * ff), BF16),
            pltpu.VMEM((chunk, 3 * ff), F32),
            pltpu.VMEM((subs, chunk, 3 * ff), BF16),
            pltpu.VMEM((rows, 2 * ff), BF16),
            pltpu.VMEM((2 * subs, chunk, LANES), F32),
            pltpu.VMEM((rows, dh), BF16),
            pltpu.VMEM((rows // 2, dh), BF16),
            pltpu.VMEM((sources * PAD, dh), BF16),
            pltpu.VMEM((slots, width), BF16),
            pltpu.VMEM((examples * share, LANES), BF16),
            pltpu.VMEM((owners, piece, LANES), BF16),
            dma((sources,)), dma((sources,)), dma((sources,)), dma((sources,)),
            dma((subs,)), dma((subs,)), dma((subs,)), dma((subs,)),
            dma((2 * subs,)), dma((2 * subs,)), dma(()), dma(()),
            dma((sources,)), dma((sources,)), dma((owners,)), dma((owners,)), dma(()),
        ],
        compiler_params=pltpu.CompilerParams(
            collective_id=0, has_side_effects=True, vmem_limit_bytes=60 * 1024 * 1024
        ),
    )(payload, pick_token, gate_w[0], up_w[0], down_w[0], ph)
    eg = eg.reshape(owners, 4, share, LANES)[..., :rank_size]
    return (input_grad, jnp.swapaxes(eg, 0, 1))


def solution(mesh):
    return jax.shard_map(
        per_device,
        mesh=mesh,
        in_specs=(
            P(("groups", "expert", "sub", "pair"), None),
            P(("groups", "expert", "sub", "pair"), None),
            P(("groups", "expert", "sub", "pair"), None),
            P(("groups", "expert", "sub", "pair"), None),
            P(("groups", "expert", "sub", "pair")),
            P("expert", "sub", "pair"),
            P("expert", "sub", "pair"),
            P("expert", "pair", "sub"),
            P(),
            P(None, "pair"),
        ),
        out_specs=(
            P(("groups", "expert", "sub", "pair"), None),
            P(("groups", "expert"), None, ("sub", "pair"), None),
        ),
        check_vma=False,
    )
```

```python
import functools

import jax
import jax.numpy as jnp
from jax import lax
from jax.experimental import pallas as pl
from jax.experimental.pallas import tpu as pltpu
from jax.sharding import PartitionSpec as P

CAP = 10
PAD = 16
GROUP = 8
BLOCK = CAP * GROUP
LANES = 128
MESH = pl.DeviceIdType.MESH
F32 = jnp.float32
BF16 = jnp.bfloat16
NT = (((1,), (1,)), ((), ()))
TN = (((0,), (0,)), ((), ()))


def dot(a, b, dims=(((1,), (0,)), ((), ()))):
    return lax.dot_general(a, b, dims, preferred_element_type=F32)


def pack_matrix(rows, cols):
    i = lax.broadcasted_iota(jnp.int32, (rows, cols), 0)
    k = lax.broadcasted_iota(jnp.int32, (rows, cols), 1)
    hit = (k // PAD == i // CAP) & (k % PAD == i % CAP)
    return jnp.where(hit, 1.0, 0.0).astype(BF16)


def kernel(
    owners, subs, rank_size,
    routes_t, weight_t, example, tokens, out_grad, gate_in, up_in, down_in, proj, ph,
    ret_out, pick_out, eg_out,
    tok, og, gate, up, down, pj, px, pz, bufx, bufz, compx, compz,
    gu_send, gu_own, gu_buf, hg_send, hg_own, hg_buf, gbuf, hp_buf, rp_in, ret_buf,
    gs, eg_buf,
    load_sem, x_send, x_recv, z_send, z_recv, fx_send, fx_recv, fz_send, fz_recv,
    gu_ss, gu_rs, hg_ss, hg_rs, g_ss, g_rs, h_ss, h_rs, p_ss, p_rs, r_ss, r_rs, e_ss, e_rs,
):
    ei, si, pi = lax.axis_index("expert"), lax.axis_index("sub"), lax.axis_index("pair")
    other = 1 - pi
    sources = owners * subs
    me = ei * subs + si
    rows = compx.shape[0]
    half = rows // 2
    chunk = rows // subs
    dh = compx.shape[1]
    zw = compz.shape[1]
    ff = gate.shape[1]

    loads = [
        pltpu.make_async_copy(a, b, load_sem.at[k])
        for k, (a, b) in enumerate(
            [(tokens, tok), (out_grad, og), (proj, pj), (gate_in, gate), (up_in, up), (down_in, down)]
        )
    ]
    for load in loads:
        load.start()

    barrier = pltpu.get_barrier_semaphore()

    def greet(d, c):
        j = lax.rem(me + d, sources)
        pl.semaphore_signal(
            barrier, 1, device_id={"expert": j // subs, "sub": j % subs}, device_id_type=MESH
        )
        return c

    lax.fori_loop(1, sources, greet, 0)
    for d in range(subs):
        pl.semaphore_signal(
            barrier, 1, device_id={"sub": lax.rem(si + d, subs), "pair": other}, device_id_type=MESH
        )

    tokens_here = tok.shape[0]
    named = [(routes_t[...] == e) for e in range(owners)]
    taken = jnp.concatenate(
        [jnp.sum(jnp.where(n, 1.0, 0.0), axis=0, keepdims=True) for n in named], axis=0
    )
    weights = weight_t[...].astype(F32)
    chosen = [jnp.sum(jnp.where(n, weights, 0.0), axis=0, keepdims=True) for n in named]
    lower = lax.broadcasted_iota(jnp.int32, (tokens_here, tokens_here), 0)
    upper = lax.broadcasted_iota(jnp.int32, (tokens_here, tokens_here), 1)
    before = dot(taken.astype(BF16), jnp.where(lower < upper, 1.0, 0.0).astype(BF16))
    slot = lax.broadcasted_iota(jnp.int32, (PAD, tokens_here), 0).astype(F32)
    hits, slot_weights, slot_codes = [], [], []
    codes = (example[...] + 1).astype(F32)
    for e in range(owners):
        hit = jnp.where((before[e : e + 1] == slot) & (taken[e : e + 1] > 0.5), 1.0, 0.0)
        hits.append(hit)
        slot_weights.append(jnp.sum(hit * chosen[e], axis=1, keepdims=True))
        slot_codes.append(jnp.sum(hit * codes, axis=1, keepdims=True))
    pick = jnp.concatenate(hits, axis=0).astype(BF16)
    slot_weight = jnp.concatenate(slot_weights, axis=0)
    slot_code = jnp.concatenate(slot_codes, axis=0)
    pick_out[...] = pick
    loads[0].wait()
    px[...] = dot(pick, tok[...]).astype(BF16)
    pl.semaphore_wait(barrier, sources - 1 + subs)

    def padded(j):
        return pl.ds(pl.multiple_of(j * PAD, PAD), PAD)

    def rows_to(d, pack, buf, ss, rs):
        j = lax.rem(me + d, sources)
        e, s = j // subs, j % subs
        wide = buf.shape[2]
        return pltpu.make_async_remote_copy(
            src_ref=pack.at[padded(e), pl.ds(pl.multiple_of(s * wide, LANES), wide)],
            dst_ref=buf.at[pi, padded(me)],
            send_sem=ss.at[j],
            recv_sem=rs.at[me],
            device_id={"expert": e, "sub": s},
            device_id_type=MESH,
        )

    def forward(j, half_at, buf, ss, rs):
        return pltpu.make_async_remote_copy(
            src_ref=buf.at[half_at, padded(j)],
            dst_ref=buf.at[half_at, padded(j)],
            send_sem=ss.at[j],
            recv_sem=rs.at[j],
            device_id={"pair": other},
            device_id_type=MESH,
        )

    def send_rows(pack, buf, ss, rs, fss, frs):
        def body(d, c):
            rows_to(d, pack, buf, ss, rs).start()
            return c

        lax.fori_loop(1, sources, body, 0)
        wide = buf.shape[2]
        buf[pi, padded(me), :] = pack[padded(ei), pl.ds(pl.multiple_of(si * wide, LANES), wide)]
        forward(me, pi, buf, fss, frs).start()

    send_rows(px, bufx, x_send, x_recv, fx_send, fx_recv)

    loads[1].wait()
    scaled = (slot_weight * dot(pick, og[...])).astype(BF16)
    loads[2].wait()
    projected = dot(scaled, pj[...], NT).astype(BF16)
    lane = lax.broadcasted_iota(jnp.int32, (owners * PAD, LANES - rank_size), 1)
    extra = jnp.concatenate(
        [projected, jnp.where(lane == 0, slot_code, 0.0).astype(BF16)], axis=1
    )
    for s in range(subs):
        pz[:, s * zw : s * zw + dh] = scaled[:, s * dh : (s + 1) * dh]
        pz[:, s * zw + dh : (s + 1) * zw] = extra
    send_rows(pz, bufz, z_send, z_recv, fz_send, fz_recv)

    squeeze = pack_matrix(BLOCK, GROUP * PAD)

    def compact(half_at, buf, comp):
        def body(g, c):
            part = buf[half_at, pl.ds(pl.multiple_of(g * GROUP * PAD, GROUP * PAD), GROUP * PAD), :]
            at = pl.multiple_of(half_at * half + g * BLOCK, PAD)
            comp[pl.ds(at, BLOCK), :] = dot(squeeze, part).astype(BF16)
            return c

        lax.fori_loop(0, sources // GROUP, body, 0)

    def take_rows(buf, comp, ss, rs, fss, frs):
        def pass_on(d, c):
            j = lax.rem(me - d + sources, sources)
            pltpu.make_async_remote_copy(
                src_ref=buf.at[pi, padded(j)],
                dst_ref=buf.at[pi, padded(j)],
                send_sem=ss.at[j],
                recv_sem=rs.at[j],
                device_id={"expert": j // subs, "sub": j % subs},
                device_id_type=MESH,
            ).wait_recv()
            forward(j, pi, buf, fss, frs).start()
            return c

        lax.fori_loop(1, sources, pass_on, 0)
        compact(pi, buf, comp)

        def take_pass(j, c):
            forward(j, other, buf, fss, frs).wait_recv()
            return c

        lax.fori_loop(0, sources, take_pass, 0)
        compact(other, buf, comp)

    def gate_up(at, out, to):
        x = compx[pl.ds(at, BLOCK), :]
        out[pl.ds(to, BLOCK), 0:ff] = dot(x, gate[...]).astype(out.dtype)
        out[pl.ds(to, BLOCK), ff : 2 * ff] = dot(x, up[...]).astype(out.dtype)

    def grad(at, out, to):
        z = compz[pl.ds(at, BLOCK), 0:dh]
        out[pl.ds(to, BLOCK), :] = dot(z, down[...], NT).astype(out.dtype)

    def share_copy(d, src, buf, ss, rs, came):
        s = lax.rem(si + d, subs)
        at = s if came else si
        return pltpu.make_async_remote_copy(
            src_ref=buf.at[at] if came else src.at[pl.ds(pl.multiple_of(s * chunk, PAD), chunk)],
            dst_ref=buf.at[at],
            send_sem=ss.at[s],
            recv_sem=rs.at[at],
            device_id={"sub": s},
            device_id_type=MESH,
        )

    def exchange(work, src, own, buf, ss, rs):
        for d in range(1, subs):
            base = lax.rem(si + d, subs) * chunk

            def send_block(b, c):
                at = pl.multiple_of(base + b * BLOCK, PAD)
                work(at, src, at)
                return c

            lax.fori_loop(0, chunk // BLOCK, send_block, 0)
            share_copy(d, src, buf, ss, rs, False).start()

        def own_block(b, c):
            at = pl.multiple_of(si * chunk + b * BLOCK, PAD)
            work(at, own, pl.multiple_of(b * BLOCK, PAD))
            return c

        lax.fori_loop(0, chunk // BLOCK, own_block, 0)

    def summed(own, buf, to, k):
        v = own[pl.ds(to, BLOCK), k * ff : (k + 1) * ff]
        for d in range(1, subs):
            s = lax.rem(si + d, subs)
            v = v + buf[s, pl.ds(to, BLOCK), k * ff : (k + 1) * ff].astype(F32)
        return v

    take_rows(bufx, compx, x_send, x_recv, fx_send, fx_recv)
    loads[3].wait()
    loads[4].wait()
    exchange(gate_up, gu_send, gu_own, gu_buf, gu_ss, gu_rs)
    take_rows(bufz, compz, z_send, z_recv, fz_send, fz_recv)
    loads[5].wait()
    exchange(grad, hg_send, hg_own, hg_buf, hg_ss, hg_rs)

    hp_me = si * 2 + pi
    for d in range(1, subs):
        share_copy(d, gu_send, gu_buf, gu_ss, gu_rs, True).wait_recv()

    def hidden_block(b, c):
        to = pl.multiple_of(b * BLOCK, PAD)
        g, u = summed(gu_own, gu_buf, to, 0), summed(gu_own, gu_buf, to, 1)
        gu_own[pl.ds(to, BLOCK), 0:ff] = g
        gu_own[pl.ds(to, BLOCK), ff : 2 * ff] = u
        hidden = (g * (1.0 / (1.0 + jnp.exp(-g))) * u).astype(BF16)
        v = dot(hidden, ph[...], NT)
        hp_buf[hp_me, pl.ds(to, BLOCK), :] = jnp.concatenate(
            [v, jnp.zeros((BLOCK, LANES - rank_size), F32)], axis=1
        )
        return c

    lax.fori_loop(0, chunk // BLOCK, hidden_block, 0)

    def h_copy(d, came):
        q = lax.rem(hp_me + d, 2 * subs)
        at = q if came else hp_me
        return pltpu.make_async_remote_copy(
            src_ref=hp_buf.at[at],
            dst_ref=hp_buf.at[at],
            send_sem=h_ss.at[q],
            recv_sem=h_rs.at[at],
            device_id={"sub": q // 2, "pair": q % 2},
            device_id_type=MESH,
        )

    for d in range(1, 2 * subs):
        h_copy(d, False).start()
    for d in range(1, subs):
        share_copy(d, hg_send, hg_buf, hg_ss, hg_rs, True).wait_recv()

    def act_block(b, c):
        to = pl.multiple_of(b * BLOCK, PAD)
        g, u = gu_own[pl.ds(to, BLOCK), 0:ff], gu_own[pl.ds(to, BLOCK), ff : 2 * ff]
        h = summed(hg_own, hg_buf, to, 0)
        sig = 1.0 / (1.0 + jnp.exp(-g))
        at = pl.multiple_of(si * chunk + b * BLOCK, PAD)
        gbuf[pl.ds(at, BLOCK), 0:ff] = (h * u * sig * (1.0 + g * (1.0 - sig))).astype(BF16)
        gbuf[pl.ds(at, BLOCK), ff : 2 * ff] = (h * (g * sig)).astype(BF16)
        return c

    lax.fori_loop(0, chunk // BLOCK, act_block, 0)

    def g_copy(d, came):
        s = lax.rem(si + d, subs)
        at = s if came else si
        span = gbuf.at[pl.ds(pl.multiple_of(at * chunk, PAD), chunk)]
        return pltpu.make_async_remote_copy(
            src_ref=span,
            dst_ref=span,
            send_sem=g_ss.at[s],
            recv_sem=g_rs.at[at],
            device_id={"sub": s},
            device_id_type=MESH,
        )

    for d in range(1, subs):
        g_copy(d, False).start()

    rp, ret_send = compx, bufx.at[other]

    def swap(s):
        span = pl.ds(pl.multiple_of(s * chunk, PAD), chunk)
        return pltpu.make_async_remote_copy(
            src_ref=rp.at[span],
            dst_ref=rp_in.at[pl.ds(pl.multiple_of(s % (subs // 2) * chunk, PAD), chunk)],
            send_sem=p_ss.at[s],
            recv_sem=p_rs.at[s],
            device_id={"pair": other},
            device_id_type=MESH,
        )

    def back(j, came):
        at_e = j // subs if came else ei
        at_s = j % subs if came else si
        return pltpu.make_async_remote_copy(
            src_ref=ret_send.at[padded(j)],
            dst_ref=ret_buf.at[padded(at_e), pl.ds(pl.multiple_of(at_s * dh, LANES), dh)],
            send_sem=r_ss.at[j],
            recv_sem=r_rs.at[j if came else me],
            device_id={"expert": j // subs, "sub": j % subs},
            device_id_type=MESH,
        )

    per_chunk = chunk // CAP

    def route_chunk(s):
        def body(b, c):
            at = pl.multiple_of(s * chunk + b * BLOCK, PAD)
            v = dot(gbuf[pl.ds(at, BLOCK), 0:ff], gate[...], NT)
            v = v + dot(gbuf[pl.ds(at, BLOCK), ff : 2 * ff], up[...], NT)
            rp[pl.ds(at, BLOCK), :] = v.astype(BF16)
            return c

        lax.fori_loop(0, chunk // BLOCK, body, 0)
        first = s * per_chunk - pi * sources

        @pl.when(s * 2 // subs == other)
        def _():
            swap(s).start()

        @pl.when(s * 2 // subs == pi)
        def _():
            swap(s).wait_recv()

            def sum_block(b, c):
                at = pl.multiple_of(s * chunk + b * BLOCK, PAD)
                came = pl.multiple_of(s % (subs // 2) * chunk + b * BLOCK, PAD)
                v = rp[pl.ds(at, BLOCK), :].astype(F32) + rp_in[pl.ds(came, BLOCK), :].astype(F32)
                put = pl.multiple_of((first + b * GROUP) * PAD, GROUP * PAD)
                ret_send[pl.ds(put, GROUP * PAD), :] = dot(squeeze, v.astype(BF16), TN).astype(BF16)
                return c

            lax.fori_loop(0, chunk // BLOCK, sum_block, 0)

            def start_back(i, c):
                j = first + lax.rem(me + 1 + i, per_chunk)

                @pl.when(j != me)
                def _():
                    back(j, False).start()

                @pl.when(j == me)
                def _():
                    ret_buf[padded(ei), pl.ds(pl.multiple_of(si * dh, LANES), dh)] = ret_send[
                        padded(me), :
                    ]

                return c

            lax.fori_loop(0, per_chunk, start_back, 0)

    route_chunk(si)

    for d in range(1, 2 * subs):
        h_copy(d, True).wait_recv()
    share = rank_size // (2 * subs)
    spread_cols = gs.shape[0]
    row = lax.broadcasted_iota(jnp.int32, (LANES, spread_cols), 0)
    col = lax.broadcasted_iota(jnp.int32, (LANES, spread_cols), 1)
    repeat = jnp.where(row == hp_me * share + col % share, 1.0, 0.0).astype(BF16)
    want = (
        lax.broadcasted_iota(jnp.int32, (BLOCK, spread_cols), 1) // share + 1
    ).astype(F32)

    def example_block(b, acc):
        at = pl.multiple_of(b * BLOCK, PAD)
        ex = compz[pl.ds(at, BLOCK), dh:zw]
        code = ex[:, rank_size : rank_size + 1].astype(F32)
        spread = jnp.where(code == want, dot(ex, repeat), 0.0).astype(BF16)
        s = b // (chunk // BLOCK)
        to = pl.multiple_of((b % (chunk // BLOCK)) * BLOCK, PAD)
        hp = hp_buf[2 * s, pl.ds(to, BLOCK), :] + hp_buf[2 * s + 1, pl.ds(to, BLOCK), :]
        hi = hp.astype(BF16)
        rest = hp - hi.astype(F32)
        mid = rest.astype(BF16)
        low = (rest - mid.astype(F32)).astype(BF16)
        return acc + dot(spread, hi, TN) + dot(spread, mid, TN) + dot(spread, low, TN)

    gs[...] = lax.fori_loop(
        0, rows // BLOCK, example_block, jnp.zeros((spread_cols, LANES), F32)
    ).astype(BF16)
    piece = spread_cols // owners

    def e_copy(e, came):
        return pltpu.make_async_remote_copy(
            src_ref=gs.at[pl.ds(pl.multiple_of(e * piece, PAD), piece)],
            dst_ref=eg_buf.at[e if came else ei],
            send_sem=e_ss.at[e],
            recv_sem=e_rs.at[e if came else ei],
            device_id={"expert": e},
            device_id_type=MESH,
        )

    def start_e(d, c):
        e_copy(lax.rem(ei + d, owners), False).start()
        return c

    lax.fori_loop(1, owners, start_e, 0)
    eg_buf[ei] = gs[pl.ds(pl.multiple_of(ei * piece, PAD), piece), :]

    for d in range(1, subs):
        g_copy(d, True).wait_recv()
        route_chunk(lax.rem(si + d, subs))

    def take_e(d, c):
        e_copy(lax.rem(ei + d, owners), True).wait_recv()
        return c

    lax.fori_loop(1, owners, take_e, 0)
    eg = eg_buf[...].astype(F32)
    for x in range(4):
        eg_out[x] = eg[:, x * share : (x + 1) * share, 0:rank_size]

    def sent(d, c):
        j = lax.rem(me + d, sources)
        rows_to(d, px, bufx, x_send, x_recv).wait_send()
        rows_to(d, pz, bufz, z_send, z_recv).wait_send()
        back(j, False).wait_send()
        return c

    lax.fori_loop(1, sources, sent, 0)

    def sent_pass(j, c):
        forward(j, pi, bufx, fx_send, fx_recv).wait_send()
        forward(j, pi, bufz, fz_send, fz_recv).wait_send()
        return c

    lax.fori_loop(0, sources, sent_pass, 0)
    for d in range(1, subs):
        share_copy(d, gu_send, gu_buf, gu_ss, gu_rs, False).wait_send()
        share_copy(d, hg_send, hg_buf, hg_ss, hg_rs, False).wait_send()
        g_copy(d, False).wait_send()
    for d in range(1, 2 * subs):
        h_copy(d, False).wait_send()
    for i in range(subs // 2):
        swap(other * (subs // 2) + i).wait_send()

    def sent_e(d, c):
        e_copy(lax.rem(ei + d, owners), False).wait_send()
        return c

    lax.fori_loop(1, owners, sent_e, 0)

    def take_back(d, c):
        back(lax.rem(me + d, sources), True).wait_recv()
        return c

    lax.fori_loop(1, sources, take_back, 0)
    ret_out[...] = ret_buf[...]


def per_device(
    tokens, out_grad, routes, route_weight, example_id, gate_w, up_w, down_w, proj_grad, proj_hidden
):
    owners = lax.axis_size("expert")
    subs = lax.axis_size("sub")
    local_tokens, width = tokens.shape
    rank_size = proj_grad.shape[0]
    slots = owners * PAD
    dh = width // subs
    zw = dh + LANES
    ff = gate_w.shape[2]
    sources = owners * subs
    rows = sources * 2 * CAP
    chunk = rows // subs
    examples = 4 * owners
    share = rank_size // (2 * subs)
    piece = 4 * share
    vmem = pl.BlockSpec(memory_space=pltpu.VMEM)
    hbm = pl.BlockSpec(memory_space=pl.ANY)
    dma = pltpu.SemaphoreType.DMA

    def space(*shape, kind=BF16):
        return pltpu.VMEM(shape, kind)

    returned, pick_token, example_grads = pl.pallas_call(
        functools.partial(kernel, owners, subs, rank_size),
        out_shape=(
            jax.ShapeDtypeStruct((slots, width), BF16),
            jax.ShapeDtypeStruct((slots, local_tokens), BF16),
            jax.ShapeDtypeStruct((4, owners, share, rank_size), F32),
        ),
        in_specs=[vmem] * 3 + [hbm] * 6 + [vmem],
        out_specs=(vmem, vmem, vmem),
        scratch_shapes=[
            space(local_tokens, width),
            space(local_tokens, width),
            space(dh, ff),
            space(dh, ff),
            space(ff, dh),
            space(rank_size, width),
            space(slots, width),
            space(slots, subs * zw),
            space(2, sources * PAD, dh),
            space(2, sources * PAD, zw),
            space(rows, dh),
            space(rows, zw),
            space(rows, 2 * ff),
            space(chunk, 2 * ff, kind=F32),
            space(subs, chunk, 2 * ff),
            space(rows, ff),
            space(chunk, ff, kind=F32),
            space(subs, chunk, ff),
            space(rows, 2 * ff),
            space(2 * subs, chunk, LANES, kind=F32),
            space(rows // 2, dh),
            space(slots, width),
            space(examples * share, LANES),
            space(owners, piece, LANES),
            dma((6,)),
        ]
        + [dma((sources,))] * 8
        + [dma((subs,))] * 6
        + [dma((2 * subs,))] * 2
        + [dma((subs,))] * 2
        + [dma((sources,))] * 2
        + [dma((owners,))] * 2,
        compiler_params=pltpu.CompilerParams(
            collective_id=0, has_side_effects=True, vmem_limit_bytes=60 * 1024 * 1024
        ),
    )(
        routes.T, route_weight.T, example_id[None, :], tokens, out_grad,
        gate_w[0], up_w[0], down_w[0], proj_grad, proj_hidden,
    )
    input_grad = dot(pick_token, returned, TN).astype(BF16)
    return (input_grad, example_grads)


def solution(mesh):
    return jax.shard_map(
        per_device,
        mesh=mesh,
        in_specs=(
            P(("groups", "expert", "sub", "pair"), None),
            P(("groups", "expert", "sub", "pair"), None),
            P(("groups", "expert", "sub", "pair"), None),
            P(("groups", "expert", "sub", "pair"), None),
            P(("groups", "expert", "sub", "pair")),
            P("expert", "sub", "pair"),
            P("expert", "sub", "pair"),
            P("expert", "pair", "sub"),
            P(),
            P(None, "pair"),
        ),
        out_specs=(
            P(("groups", "expert", "sub", "pair"), None),
            P(("groups", "expert"), None, ("sub", "pair"), None),
        ),
        check_vma=False,
    )
```

```python
import functools

import jax
import jax.numpy as jnp
from jax import lax
from jax.experimental import pallas as pl
from jax.experimental.pallas import tpu as pltpu
from jax.sharding import PartitionSpec as P

CAP = 10
PAD = 16
GROUP = 8
BLOCK = CAP * GROUP
LANES = 128
MESH = pl.DeviceIdType.MESH
F32 = jnp.float32
BF16 = jnp.bfloat16
NT = (((1,), (1,)), ((), ()))
TN = (((0,), (0,)), ((), ()))


def dot(a, b, dims=(((1,), (0,)), ((), ()))):
    return lax.dot_general(a, b, dims, preferred_element_type=F32)


def pack_matrix(rows, cols):
    i = lax.broadcasted_iota(jnp.int32, (rows, cols), 0)
    k = lax.broadcasted_iota(jnp.int32, (rows, cols), 1)
    hit = (k // PAD == i // CAP) & (k % PAD == i % CAP)
    return jnp.where(hit, 1.0, 0.0).astype(BF16)


def segments(tiles):
    keep = -(-tiles * CAP // PAD)
    found = {}
    for f in range(CAP * (tiles - keep)):
        k, i = divmod(f, PAD - CAP)
        key = (k, keep + f // CAP)
        lo, _, shift = found.get(key, (CAP + i, 0, CAP + i - f % CAP))
        found[key] = (lo, CAP + i + 1, shift)
    return keep, [(k, t) + v for (k, t), v in found.items()]


def tile(k, n=1):
    return slice(k * LANES, (k + n) * LANES)


def mover(to_rows, to_step, from_rows, from_step, lo, hi, shift):
    a = lax.broadcasted_iota(jnp.int32, (to_rows, from_rows), 0)
    b = lax.broadcasted_iota(jnp.int32, (to_rows, from_rows), 1)
    within = a % to_step
    hit = (a // to_step == b // from_step) & (within - b % from_step == shift)
    return jnp.where(hit & (within >= lo) & (within < hi), 1.0, 0.0).astype(BF16)


def fold(value):
    keep, segs = segments(value.shape[1] // LANES)
    n = value.shape[0]
    parts = [value[:, tile(k)].astype(F32) for k in range(keep)]
    for k, t, lo, hi, shift in segs:
        parts[k] = parts[k] + dot(mover(n, PAD, n, PAD, lo, hi, shift), value[:, tile(t)])
    return jnp.concatenate([p.astype(BF16) for p in parts], axis=1)


def kernel(
    owners, subs, rank_size,
    routes_t, weight_t, example, tokens, out_grad, gate_in, up_in, down_in, proj, ph,
    ret_out, pick_out, eg_out,
    tok, og, gate, up, down, pj, px, pz, bufx, bufz, compx, compz,
    gu_send, gu_own, gu_buf, hg_send, hg_own, hg_buf, gbuf, hp_buf, rp_in, ret_buf,
    gs, eg_buf,
    load_sem, x_send, x_recv, z_send, z_recv, fx_send, fx_recv, fz_send, fz_recv,
    gu_ss, gu_rs, hg_ss, hg_rs, g_ss, g_rs, h_ss, h_rs, p_ss, p_rs, r_ss, r_rs, e_ss, e_rs,
):
    ei, si, pi = lax.axis_index("expert"), lax.axis_index("sub"), lax.axis_index("pair")
    other = 1 - pi
    sources = owners * subs
    me = ei * subs + si
    rows = compx.shape[0]
    half = rows // 2
    chunk = rows // subs
    dh = compx.shape[1]
    zw = compz.shape[1]
    wx, wz = bufx.shape[2], bufz.shape[2]
    ff = gate.shape[1]

    loads = [
        pltpu.make_async_copy(a, b, load_sem.at[k])
        for k, (a, b) in enumerate(
            [(tokens, tok), (out_grad, og), (proj, pj), (gate_in, gate), (up_in, up), (down_in, down)]
        )
    ]
    for load in loads:
        load.start()

    barrier = pltpu.get_barrier_semaphore()

    def greet(d, c):
        j = lax.rem(me + d, sources)
        pl.semaphore_signal(
            barrier, 1, device_id={"expert": j // subs, "sub": j % subs}, device_id_type=MESH
        )
        return c

    lax.fori_loop(1, sources, greet, 0)
    for d in range(subs):
        pl.semaphore_signal(
            barrier, 1, device_id={"sub": lax.rem(si + d, subs), "pair": other}, device_id_type=MESH
        )

    tokens_here = tok.shape[0]
    named = [(routes_t[...] == e) for e in range(owners)]
    taken = jnp.concatenate(
        [jnp.sum(jnp.where(n, 1.0, 0.0), axis=0, keepdims=True) for n in named], axis=0
    )
    weights = weight_t[...].astype(F32)
    chosen = [jnp.sum(jnp.where(n, weights, 0.0), axis=0, keepdims=True) for n in named]
    lower = lax.broadcasted_iota(jnp.int32, (tokens_here, tokens_here), 0)
    upper = lax.broadcasted_iota(jnp.int32, (tokens_here, tokens_here), 1)
    before = dot(taken.astype(BF16), jnp.where(lower < upper, 1.0, 0.0).astype(BF16))
    slot = lax.broadcasted_iota(jnp.int32, (PAD, tokens_here), 0).astype(F32)
    hits, slot_weights, slot_codes = [], [], []
    codes = (example[...] + 1).astype(F32)
    for e in range(owners):
        hit = jnp.where((before[e : e + 1] == slot) & (taken[e : e + 1] > 0.5), 1.0, 0.0)
        hits.append(hit)
        slot_weights.append(jnp.sum(hit * chosen[e], axis=1, keepdims=True))
        slot_codes.append(jnp.sum(hit * codes, axis=1, keepdims=True))
    pick = jnp.concatenate(hits, axis=0).astype(BF16)
    slot_weight = jnp.concatenate(slot_weights, axis=0)
    slot_code = jnp.concatenate(slot_codes, axis=0)
    pick_out[...] = pick
    loads[0].wait()
    picked = dot(pick, tok[...]).astype(BF16)
    for s in range(subs):
        px[:, s * wx : (s + 1) * wx] = fold(picked[:, s * dh : (s + 1) * dh])
    pl.semaphore_wait(barrier, sources - 1 + subs)

    def padded(j):
        return pl.ds(pl.multiple_of(j * PAD, PAD), PAD)

    def rows_to(d, pack, buf, ss, rs):
        j = lax.rem(me + d, sources)
        e, s = j // subs, j % subs
        wide = buf.shape[2]
        return pltpu.make_async_remote_copy(
            src_ref=pack.at[padded(e), pl.ds(pl.multiple_of(s * wide, LANES), wide)],
            dst_ref=buf.at[pi, padded(me)],
            send_sem=ss.at[j],
            recv_sem=rs.at[me],
            device_id={"expert": e, "sub": s},
            device_id_type=MESH,
        )

    def forward(j, half_at, buf, ss, rs):
        return pltpu.make_async_remote_copy(
            src_ref=buf.at[half_at, padded(j)],
            dst_ref=buf.at[half_at, padded(j)],
            send_sem=ss.at[j],
            recv_sem=rs.at[j],
            device_id={"pair": other},
            device_id_type=MESH,
        )

    def send_rows(pack, buf, ss, rs, fss, frs):
        def body(d, c):
            rows_to(d, pack, buf, ss, rs).start()
            return c

        lax.fori_loop(1, sources, body, 0)
        wide = buf.shape[2]
        buf[pi, padded(me), :] = pack[padded(ei), pl.ds(pl.multiple_of(si * wide, LANES), wide)]
        forward(me, pi, buf, fss, frs).start()

    send_rows(px, bufx, x_send, x_recv, fx_send, fx_recv)

    loads[1].wait()
    scaled = (slot_weight * dot(pick, og[...])).astype(BF16)
    loads[2].wait()
    projected = dot(scaled, pj[...], NT).astype(BF16)
    lane = lax.broadcasted_iota(jnp.int32, (owners * PAD, LANES - rank_size), 1)
    extra = jnp.concatenate(
        [projected, jnp.where(lane == 0, slot_code, 0.0).astype(BF16)], axis=1
    )
    for s in range(subs):
        pz[:, s * wz : (s + 1) * wz] = fold(
            jnp.concatenate([scaled[:, s * dh : (s + 1) * dh], extra], axis=1)
        )
    send_rows(pz, bufz, z_send, z_recv, fz_send, fz_recv)

    squeeze = pack_matrix(BLOCK, GROUP * PAD)

    def unfolders(tiles):
        return [
            (k, t, mover(BLOCK, CAP, GROUP * PAD, PAD, lo - shift, hi - shift, -shift))
            for k, t, lo, hi, shift in segments(tiles)[1]
        ]

    def compact(half_at, buf, comp, moves):
        keep = buf.shape[2] // LANES

        def body(g, c):
            part = buf[half_at, pl.ds(pl.multiple_of(g * GROUP * PAD, GROUP * PAD), GROUP * PAD), :]
            at = pl.multiple_of(half_at * half + g * BLOCK, PAD)
            comp[pl.ds(at, BLOCK), tile(0, keep)] = dot(squeeze, part).astype(BF16)
            for t in range(keep, comp.shape[1] // LANES):
                v = sum(dot(m, part[:, tile(k)]) for k, to, m in moves if to == t)
                comp[pl.ds(at, BLOCK), tile(t)] = v.astype(BF16)
            return c

        lax.fori_loop(0, sources // GROUP, body, 0)

    def take_rows(buf, comp, ss, rs, fss, frs):
        moves = unfolders(comp.shape[1] // LANES)

        def pass_on(d, c):
            j = lax.rem(me - d + sources, sources)
            pltpu.make_async_remote_copy(
                src_ref=buf.at[pi, padded(j)],
                dst_ref=buf.at[pi, padded(j)],
                send_sem=ss.at[j],
                recv_sem=rs.at[j],
                device_id={"expert": j // subs, "sub": j % subs},
                device_id_type=MESH,
            ).wait_recv()
            forward(j, pi, buf, fss, frs).start()
            return c

        lax.fori_loop(1, sources, pass_on, 0)
        compact(pi, buf, comp, moves)

        def take_pass(j, c):
            forward(j, other, buf, fss, frs).wait_recv()
            return c

        lax.fori_loop(0, sources, take_pass, 0)
        compact(other, buf, comp, moves)

    def gate_up(at, out, to):
        x = compx[pl.ds(at, BLOCK), :]
        out[pl.ds(to, BLOCK), 0:ff] = dot(x, gate[...]).astype(out.dtype)
        out[pl.ds(to, BLOCK), ff : 2 * ff] = dot(x, up[...]).astype(out.dtype)

    def grad(at, out, to):
        z = compz[pl.ds(at, BLOCK), 0:dh]
        out[pl.ds(to, BLOCK), :] = dot(z, down[...], NT).astype(out.dtype)

    def share_copy(d, src, buf, ss, rs, came):
        s = lax.rem(si + d, subs)
        at = s if came else si
        return pltpu.make_async_remote_copy(
            src_ref=buf.at[at] if came else src.at[pl.ds(pl.multiple_of(s * chunk, PAD), chunk)],
            dst_ref=buf.at[at],
            send_sem=ss.at[s],
            recv_sem=rs.at[at],
            device_id={"sub": s},
            device_id_type=MESH,
        )

    def exchange(work, src, own, buf, ss, rs):
        for d in range(1, subs):
            base = lax.rem(si + d, subs) * chunk

            def send_block(b, c):
                at = pl.multiple_of(base + b * BLOCK, PAD)
                work(at, src, at)
                return c

            lax.fori_loop(0, chunk // BLOCK, send_block, 0)
            share_copy(d, src, buf, ss, rs, False).start()

        def own_block(b, c):
            at = pl.multiple_of(si * chunk + b * BLOCK, PAD)
            work(at, own, pl.multiple_of(b * BLOCK, PAD))
            return c

        lax.fori_loop(0, chunk // BLOCK, own_block, 0)

    def summed(own, buf, to, k):
        v = own[pl.ds(to, BLOCK), k * ff : (k + 1) * ff]
        for d in range(1, subs):
            s = lax.rem(si + d, subs)
            v = v + buf[s, pl.ds(to, BLOCK), k * ff : (k + 1) * ff].astype(F32)
        return v

    take_rows(bufx, compx, x_send, x_recv, fx_send, fx_recv)
    loads[3].wait()
    loads[4].wait()
    exchange(gate_up, gu_send, gu_own, gu_buf, gu_ss, gu_rs)
    take_rows(bufz, compz, z_send, z_recv, fz_send, fz_recv)
    loads[5].wait()
    exchange(grad, hg_send, hg_own, hg_buf, hg_ss, hg_rs)

    hp_me = si * 2 + pi
    for d in range(1, subs):
        share_copy(d, gu_send, gu_buf, gu_ss, gu_rs, True).wait_recv()

    def hidden_block(b, c):
        to = pl.multiple_of(b * BLOCK, PAD)
        g, u = summed(gu_own, gu_buf, to, 0), summed(gu_own, gu_buf, to, 1)
        gu_own[pl.ds(to, BLOCK), 0:ff] = g
        gu_own[pl.ds(to, BLOCK), ff : 2 * ff] = u
        hidden = (g * (1.0 / (1.0 + jnp.exp(-g))) * u).astype(BF16)
        v = dot(hidden, ph[...], NT)
        hp_buf[hp_me, pl.ds(to, BLOCK), :] = jnp.concatenate(
            [v, jnp.zeros((BLOCK, LANES - rank_size), F32)], axis=1
        )
        return c

    lax.fori_loop(0, chunk // BLOCK, hidden_block, 0)

    def h_copy(d, came):
        q = lax.rem(hp_me + d, 2 * subs)
        at = q if came else hp_me
        return pltpu.make_async_remote_copy(
            src_ref=hp_buf.at[at],
            dst_ref=hp_buf.at[at],
            send_sem=h_ss.at[q],
            recv_sem=h_rs.at[at],
            device_id={"sub": q // 2, "pair": q % 2},
            device_id_type=MESH,
        )

    for d in range(1, 2 * subs):
        h_copy(d, False).start()
    for d in range(1, subs):
        share_copy(d, hg_send, hg_buf, hg_ss, hg_rs, True).wait_recv()

    def act_block(b, c):
        to = pl.multiple_of(b * BLOCK, PAD)
        g, u = gu_own[pl.ds(to, BLOCK), 0:ff], gu_own[pl.ds(to, BLOCK), ff : 2 * ff]
        h = summed(hg_own, hg_buf, to, 0)
        sig = 1.0 / (1.0 + jnp.exp(-g))
        at = pl.multiple_of(si * chunk + b * BLOCK, PAD)
        gbuf[pl.ds(at, BLOCK), 0:ff] = (h * u * sig * (1.0 + g * (1.0 - sig))).astype(BF16)
        gbuf[pl.ds(at, BLOCK), ff : 2 * ff] = (h * (g * sig)).astype(BF16)
        return c

    lax.fori_loop(0, chunk // BLOCK, act_block, 0)

    def g_copy(d, came):
        s = lax.rem(si + d, subs)
        at = s if came else si
        span = gbuf.at[pl.ds(pl.multiple_of(at * chunk, PAD), chunk)]
        return pltpu.make_async_remote_copy(
            src_ref=span,
            dst_ref=span,
            send_sem=g_ss.at[s],
            recv_sem=g_rs.at[at],
            device_id={"sub": s},
            device_id_type=MESH,
        )

    for d in range(1, subs):
        g_copy(d, False).start()

    rp, ret_send = compx, bufx.at[other]

    def swap(s):
        span = pl.ds(pl.multiple_of(s * chunk, PAD), chunk)
        return pltpu.make_async_remote_copy(
            src_ref=rp.at[span],
            dst_ref=rp_in.at[pl.ds(pl.multiple_of(s % (subs // 2) * chunk, PAD), chunk)],
            send_sem=p_ss.at[s],
            recv_sem=p_rs.at[s],
            device_id={"pair": other},
            device_id_type=MESH,
        )

    def back(j, came):
        at_e = j // subs if came else ei
        at_s = j % subs if came else si
        return pltpu.make_async_remote_copy(
            src_ref=ret_send.at[padded(j)],
            dst_ref=ret_buf.at[padded(at_e), pl.ds(pl.multiple_of(at_s * wx, LANES), wx)],
            send_sem=r_ss.at[j],
            recv_sem=r_rs.at[j if came else me],
            device_id={"expert": j // subs, "sub": j % subs},
            device_id_type=MESH,
        )

    per_chunk = chunk // CAP

    def route_chunk(s):
        def body(b, c):
            at = pl.multiple_of(s * chunk + b * BLOCK, PAD)
            v = dot(gbuf[pl.ds(at, BLOCK), 0:ff], gate[...], NT)
            v = v + dot(gbuf[pl.ds(at, BLOCK), ff : 2 * ff], up[...], NT)
            rp[pl.ds(at, BLOCK), :] = v.astype(BF16)
            return c

        lax.fori_loop(0, chunk // BLOCK, body, 0)
        first = s * per_chunk - pi * sources

        @pl.when(s * 2 // subs == other)
        def _():
            swap(s).start()

        @pl.when(s * 2 // subs == pi)
        def _():
            swap(s).wait_recv()

            def sum_block(b, c):
                at = pl.multiple_of(s * chunk + b * BLOCK, PAD)
                came = pl.multiple_of(s % (subs // 2) * chunk + b * BLOCK, PAD)
                v = rp[pl.ds(at, BLOCK), :].astype(F32) + rp_in[pl.ds(came, BLOCK), :].astype(F32)
                put = pl.multiple_of((first + b * GROUP) * PAD, GROUP * PAD)
                v = v.astype(BF16)
                keep = wx // LANES
                for k in range(keep):
                    w = dot(squeeze, v[:, tile(k)], TN)
                    for at_k, t, m in unfolders(dh // LANES):
                        if at_k == k:
                            w = w + dot(m, v[:, tile(t)], TN)
                    ret_send[pl.ds(put, GROUP * PAD), tile(k)] = w.astype(BF16)
                return c

            lax.fori_loop(0, chunk // BLOCK, sum_block, 0)

            def start_back(i, c):
                j = first + lax.rem(me + 1 + i, per_chunk)

                @pl.when(j != me)
                def _():
                    back(j, False).start()

                @pl.when(j == me)
                def _():
                    ret_buf[padded(ei), pl.ds(pl.multiple_of(si * wx, LANES), wx)] = ret_send[
                        padded(me), :
                    ]

                return c

            lax.fori_loop(0, per_chunk, start_back, 0)

    route_chunk(si)

    for d in range(1, 2 * subs):
        h_copy(d, True).wait_recv()
    share = rank_size // (2 * subs)
    spread_cols = gs.shape[0]
    row = lax.broadcasted_iota(jnp.int32, (LANES, spread_cols), 0)
    col = lax.broadcasted_iota(jnp.int32, (LANES, spread_cols), 1)
    repeat = jnp.where(row == hp_me * share + col % share, 1.0, 0.0).astype(BF16)
    want = (
        lax.broadcasted_iota(jnp.int32, (BLOCK, spread_cols), 1) // share + 1
    ).astype(F32)

    def example_block(b, acc):
        at = pl.multiple_of(b * BLOCK, PAD)
        ex = compz[pl.ds(at, BLOCK), dh:zw]
        code = ex[:, rank_size : rank_size + 1].astype(F32)
        spread = jnp.where(code == want, dot(ex, repeat), 0.0).astype(BF16)
        s = b // (chunk // BLOCK)
        to = pl.multiple_of((b % (chunk // BLOCK)) * BLOCK, PAD)
        hp = hp_buf[2 * s, pl.ds(to, BLOCK), :] + hp_buf[2 * s + 1, pl.ds(to, BLOCK), :]
        hi = hp.astype(BF16)
        rest = hp - hi.astype(F32)
        mid = rest.astype(BF16)
        low = (rest - mid.astype(F32)).astype(BF16)
        return acc + dot(spread, hi, TN) + dot(spread, mid, TN) + dot(spread, low, TN)

    gs[...] = lax.fori_loop(
        0, rows // BLOCK, example_block, jnp.zeros((spread_cols, LANES), F32)
    ).astype(BF16)
    piece = spread_cols // owners

    def e_copy(e, came):
        return pltpu.make_async_remote_copy(
            src_ref=gs.at[pl.ds(pl.multiple_of(e * piece, PAD), piece)],
            dst_ref=eg_buf.at[e if came else ei],
            send_sem=e_ss.at[e],
            recv_sem=e_rs.at[e if came else ei],
            device_id={"expert": e},
            device_id_type=MESH,
        )

    def start_e(d, c):
        e_copy(lax.rem(ei + d, owners), False).start()
        return c

    lax.fori_loop(1, owners, start_e, 0)
    eg_buf[ei] = gs[pl.ds(pl.multiple_of(ei * piece, PAD), piece), :]

    for d in range(1, subs):
        g_copy(d, True).wait_recv()
        route_chunk(lax.rem(si + d, subs))

    def take_e(d, c):
        e_copy(lax.rem(ei + d, owners), True).wait_recv()
        return c

    lax.fori_loop(1, owners, take_e, 0)
    eg = eg_buf[...].astype(F32)
    for x in range(4):
        eg_out[x] = eg[:, x * share : (x + 1) * share, 0:rank_size]

    def sent(d, c):
        j = lax.rem(me + d, sources)
        rows_to(d, px, bufx, x_send, x_recv).wait_send()
        rows_to(d, pz, bufz, z_send, z_recv).wait_send()
        back(j, False).wait_send()
        return c

    lax.fori_loop(1, sources, sent, 0)

    def sent_pass(j, c):
        forward(j, pi, bufx, fx_send, fx_recv).wait_send()
        forward(j, pi, bufz, fz_send, fz_recv).wait_send()
        return c

    lax.fori_loop(0, sources, sent_pass, 0)
    for d in range(1, subs):
        share_copy(d, gu_send, gu_buf, gu_ss, gu_rs, False).wait_send()
        share_copy(d, hg_send, hg_buf, hg_ss, hg_rs, False).wait_send()
        g_copy(d, False).wait_send()
    for d in range(1, 2 * subs):
        h_copy(d, False).wait_send()
    for i in range(subs // 2):
        swap(other * (subs // 2) + i).wait_send()

    def sent_e(d, c):
        e_copy(lax.rem(ei + d, owners), False).wait_send()
        return c

    lax.fori_loop(1, owners, sent_e, 0)

    def take_back(d, c):
        back(lax.rem(me + d, sources), True).wait_recv()
        return c

    lax.fori_loop(1, sources, take_back, 0)
    keep, segs = segments(dh // LANES)
    slots = ret_buf.shape[0]
    moves = [
        (k, t, mover(slots, PAD, slots, PAD, lo - shift, hi - shift, -shift))
        for k, t, lo, hi, shift in segs
    ]
    for s in range(subs):
        ret_out[:, s * dh : s * dh + wx] = ret_buf[:, s * wx : (s + 1) * wx]
        for to in range(keep, dh // LANES):
            v = sum(
                dot(m, ret_buf[:, s * wx + k * LANES : s * wx + (k + 1) * LANES])
                for k, t, m in moves
                if t == to
            )
            ret_out[:, s * dh + to * LANES : s * dh + (to + 1) * LANES] = v.astype(BF16)


def per_device(
    tokens, out_grad, routes, route_weight, example_id, gate_w, up_w, down_w, proj_grad, proj_hidden
):
    owners = lax.axis_size("expert")
    subs = lax.axis_size("sub")
    local_tokens, width = tokens.shape
    rank_size = proj_grad.shape[0]
    slots = owners * PAD
    dh = width // subs
    zw = dh + LANES
    wx, wz = segments(dh // LANES)[0] * LANES, segments(zw // LANES)[0] * LANES
    ff = gate_w.shape[2]
    sources = owners * subs
    rows = sources * 2 * CAP
    chunk = rows // subs
    examples = 4 * owners
    share = rank_size // (2 * subs)
    piece = 4 * share
    vmem = pl.BlockSpec(memory_space=pltpu.VMEM)
    hbm = pl.BlockSpec(memory_space=pl.ANY)
    dma = pltpu.SemaphoreType.DMA

    def space(*shape, kind=BF16):
        return pltpu.VMEM(shape, kind)

    returned, pick_token, example_grads = pl.pallas_call(
        functools.partial(kernel, owners, subs, rank_size),
        out_shape=(
            jax.ShapeDtypeStruct((slots, width), BF16),
            jax.ShapeDtypeStruct((slots, local_tokens), BF16),
            jax.ShapeDtypeStruct((4, owners, share, rank_size), F32),
        ),
        in_specs=[vmem] * 3 + [hbm] * 6 + [vmem],
        out_specs=(vmem, vmem, vmem),
        scratch_shapes=[
            space(local_tokens, width),
            space(local_tokens, width),
            space(dh, ff),
            space(dh, ff),
            space(ff, dh),
            space(rank_size, width),
            space(slots, subs * wx),
            space(slots, subs * wz),
            space(2, sources * PAD, wx),
            space(2, sources * PAD, wz),
            space(rows, dh),
            space(rows, zw),
            space(rows, 2 * ff),
            space(chunk, 2 * ff, kind=F32),
            space(subs, chunk, 2 * ff),
            space(rows, ff),
            space(chunk, ff, kind=F32),
            space(subs, chunk, ff),
            space(rows, 2 * ff),
            space(2 * subs, chunk, LANES, kind=F32),
            space(rows // 2, dh),
            space(slots, subs * wx),
            space(examples * share, LANES),
            space(owners, piece, LANES),
            dma((6,)),
        ]
        + [dma((sources,))] * 8
        + [dma((subs,))] * 6
        + [dma((2 * subs,))] * 2
        + [dma((subs,))] * 2
        + [dma((sources,))] * 2
        + [dma((owners,))] * 2,
        compiler_params=pltpu.CompilerParams(
            collective_id=0, has_side_effects=True, vmem_limit_bytes=60 * 1024 * 1024
        ),
    )(
        routes.T, route_weight.T, example_id[None, :], tokens, out_grad,
        gate_w[0], up_w[0], down_w[0], proj_grad, proj_hidden,
    )
    input_grad = dot(pick_token, returned, TN).astype(BF16)
    return (input_grad, example_grads)


def solution(mesh):
    return jax.shard_map(
        per_device,
        mesh=mesh,
        in_specs=(
            P(("groups", "expert", "sub", "pair"), None),
            P(("groups", "expert", "sub", "pair"), None),
            P(("groups", "expert", "sub", "pair"), None),
            P(("groups", "expert", "sub", "pair"), None),
            P(("groups", "expert", "sub", "pair")),
            P("expert", "sub", "pair"),
            P("expert", "sub", "pair"),
            P("expert", "pair", "sub"),
            P(),
            P(None, "pair"),
        ),
        out_specs=(
            P(("groups", "expert", "sub", "pair"), None),
            P(("groups", "expert"), None, ("sub", "pair"), None),
        ),
        check_vma=False,
    )
```

```python
import functools

import jax
import jax.numpy as jnp
from jax import lax
from jax.experimental import pallas as pl
from jax.experimental.pallas import tpu as pltpu
from jax.sharding import PartitionSpec as P

CAP = 10
PAD = 16
GROUP = 8
BLOCK = CAP * GROUP
LANES = 128
MESH = pl.DeviceIdType.MESH
F32 = jnp.float32
BF16 = jnp.bfloat16
NT = (((1,), (1,)), ((), ()))
TN = (((0,), (0,)), ((), ()))


def dot(a, b, dims=(((1,), (0,)), ((), ()))):
    return lax.dot_general(a, b, dims, preferred_element_type=F32)


def pack_matrix(rows, cols):
    i = lax.broadcasted_iota(jnp.int32, (rows, cols), 0)
    k = lax.broadcasted_iota(jnp.int32, (rows, cols), 1)
    hit = (k // PAD == i // CAP) & (k % PAD == i % CAP)
    return jnp.where(hit, 1.0, 0.0).astype(BF16)


def segments(tiles):
    keep = -(-tiles * CAP // PAD)
    found = {}
    for f in range(CAP * (tiles - keep)):
        k, i = divmod(f, PAD - CAP)
        key = (k, keep + f // CAP)
        lo, _, shift = found.get(key, (CAP + i, 0, CAP + i - f % CAP))
        found[key] = (lo, CAP + i + 1, shift)
    return keep, [(k, t) + v for (k, t), v in found.items()]


def tile(k, n=1):
    return slice(k * LANES, (k + n) * LANES)


def mover(to_rows, to_step, from_rows, from_step, lo, hi, shift):
    a = lax.broadcasted_iota(jnp.int32, (to_rows, from_rows), 0)
    b = lax.broadcasted_iota(jnp.int32, (to_rows, from_rows), 1)
    within = a % to_step
    hit = (a // to_step == b // from_step) & (within - b % from_step == shift)
    return jnp.where(hit & (within >= lo) & (within < hi), 1.0, 0.0).astype(BF16)


def fold(value):
    keep, segs = segments(value.shape[1] // LANES)
    n = value.shape[0]
    parts = [value[:, tile(k)].astype(F32) for k in range(keep)]
    for k, t, lo, hi, shift in segs:
        parts[k] = parts[k] + dot(mover(n, PAD, n, PAD, lo, hi, shift), value[:, tile(t)])
    return jnp.concatenate([p.astype(BF16) for p in parts], axis=1)


def kernel(
    owners, subs, rank_size,
    routes_t, weight_t, example, tokens, out_grad, gate_in, up_in, down_in, proj, ph,
    ret_out, pick_out, eg_out,
    tok, og, gate, up, down, pj, px, pz, bufx, bufz, compx, compz,
    gu_send, gu_own, gu_buf, hg_send, hg_own, hg_buf, gbuf, hp_buf, rp_in, ret_buf,
    gs, eg_buf,
    load_sem, x_send, x_recv, z_send, z_recv, fx_send, fx_recv, fz_send, fz_recv,
    gu_ss, gu_rs, hg_ss, hg_rs, g_ss, g_rs, h_ss, h_rs, p_ss, p_rs, r_ss, r_rs, e_ss, e_rs,
):
    ei, si, pi = lax.axis_index("expert"), lax.axis_index("sub"), lax.axis_index("pair")
    other = 1 - pi
    sources = owners * subs
    me = ei * subs + si
    rows = compx.shape[0]
    half = rows // 2
    chunk = rows // subs
    dh = compx.shape[1]
    zw = compz.shape[1]
    wx, wz = bufx.shape[2], bufz.shape[2]
    ff = gate.shape[1]

    loads = [
        pltpu.make_async_copy(a, b, load_sem.at[k])
        for k, (a, b) in enumerate(
            [(tokens, tok), (out_grad, og), (proj, pj), (gate_in, gate), (up_in, up), (down_in, down)]
        )
    ]
    loads[0].start()

    barrier = pltpu.get_barrier_semaphore()

    def greet(d, c):
        j = lax.rem(me + d, sources)
        pl.semaphore_signal(
            barrier, 1, device_id={"expert": j // subs, "sub": j % subs}, device_id_type=MESH
        )
        return c

    lax.fori_loop(1, sources, greet, 0)
    for d in range(subs):
        pl.semaphore_signal(
            barrier, 1, device_id={"sub": lax.rem(si + d, subs), "pair": other}, device_id_type=MESH
        )

    tokens_here = tok.shape[0]
    named = [(routes_t[...] == e) for e in range(owners)]
    taken = jnp.concatenate(
        [jnp.sum(jnp.where(n, 1.0, 0.0), axis=0, keepdims=True) for n in named], axis=0
    )
    weights = weight_t[...].astype(F32)
    chosen = [jnp.sum(jnp.where(n, weights, 0.0), axis=0, keepdims=True) for n in named]
    lower = lax.broadcasted_iota(jnp.int32, (tokens_here, tokens_here), 0)
    upper = lax.broadcasted_iota(jnp.int32, (tokens_here, tokens_here), 1)
    before = dot(taken.astype(BF16), jnp.where(lower < upper, 1.0, 0.0).astype(BF16))
    slot = lax.broadcasted_iota(jnp.int32, (PAD, tokens_here), 0).astype(F32)
    hits, slot_weights, slot_codes = [], [], []
    codes = (example[...] + 1).astype(F32)
    for e in range(owners):
        hit = jnp.where((before[e : e + 1] == slot) & (taken[e : e + 1] > 0.5), 1.0, 0.0)
        hits.append(hit)
        slot_weights.append(jnp.sum(hit * chosen[e], axis=1, keepdims=True))
        slot_codes.append(jnp.sum(hit * codes, axis=1, keepdims=True))
    pick = jnp.concatenate(hits, axis=0).astype(BF16)
    slot_weight = jnp.concatenate(slot_weights, axis=0)
    slot_code = jnp.concatenate(slot_codes, axis=0)
    pick_out[...] = pick
    loads[0].wait()
    for load in loads[1:]:
        load.start()
    picked = dot(pick, tok[...]).astype(BF16)
    for s in range(subs):
        px[:, s * wx : (s + 1) * wx] = fold(picked[:, s * dh : (s + 1) * dh])
    pl.semaphore_wait(barrier, sources - 1 + subs)

    def padded(j):
        return pl.ds(pl.multiple_of(j * PAD, PAD), PAD)

    def rows_to(d, pack, buf, ss, rs):
        j = lax.rem(me + d, sources)
        e, s = j // subs, j % subs
        wide = buf.shape[2]
        return pltpu.make_async_remote_copy(
            src_ref=pack.at[padded(e), pl.ds(pl.multiple_of(s * wide, LANES), wide)],
            dst_ref=buf.at[pi, padded(me)],
            send_sem=ss.at[j],
            recv_sem=rs.at[me],
            device_id={"expert": e, "sub": s},
            device_id_type=MESH,
        )

    def forward(j, half_at, buf, ss, rs):
        return pltpu.make_async_remote_copy(
            src_ref=buf.at[half_at, padded(j)],
            dst_ref=buf.at[half_at, padded(j)],
            send_sem=ss.at[j],
            recv_sem=rs.at[j],
            device_id={"pair": other},
            device_id_type=MESH,
        )

    def send_rows(pack, buf, ss, rs, fss, frs):
        def body(d, c):
            rows_to(d, pack, buf, ss, rs).start()
            return c

        lax.fori_loop(1, sources, body, 0)
        wide = buf.shape[2]
        buf[pi, padded(me), :] = pack[padded(ei), pl.ds(pl.multiple_of(si * wide, LANES), wide)]
        forward(me, pi, buf, fss, frs).start()

    send_rows(px, bufx, x_send, x_recv, fx_send, fx_recv)

    loads[1].wait()
    scaled = (slot_weight * dot(pick, og[...])).astype(BF16)
    loads[2].wait()
    projected = dot(scaled, pj[...], NT).astype(BF16)
    lane = lax.broadcasted_iota(jnp.int32, (owners * PAD, LANES - rank_size), 1)
    extra = jnp.concatenate(
        [projected, jnp.where(lane == 0, slot_code, 0.0).astype(BF16)], axis=1
    )
    for s in range(subs):
        pz[:, s * wz : (s + 1) * wz] = fold(
            jnp.concatenate([scaled[:, s * dh : (s + 1) * dh], extra], axis=1)
        )
    send_rows(pz, bufz, z_send, z_recv, fz_send, fz_recv)

    squeeze = pack_matrix(BLOCK, GROUP * PAD)

    def unfolders(tiles):
        return [
            (k, t, mover(BLOCK, CAP, GROUP * PAD, PAD, lo - shift, hi - shift, -shift))
            for k, t, lo, hi, shift in segments(tiles)[1]
        ]

    def compact(half_at, buf, comp, moves):
        keep = buf.shape[2] // LANES

        def body(g, c):
            part = buf[half_at, pl.ds(pl.multiple_of(g * GROUP * PAD, GROUP * PAD), GROUP * PAD), :]
            at = pl.multiple_of(half_at * half + g * BLOCK, PAD)
            comp[pl.ds(at, BLOCK), tile(0, keep)] = dot(squeeze, part).astype(BF16)
            for t in range(keep, comp.shape[1] // LANES):
                v = sum(dot(m, part[:, tile(k)]) for k, to, m in moves if to == t)
                comp[pl.ds(at, BLOCK), tile(t)] = v.astype(BF16)
            return c

        lax.fori_loop(0, sources // GROUP, body, 0)

    def take_rows(buf, comp, ss, rs, fss, frs):
        moves = unfolders(comp.shape[1] // LANES)

        def pass_on(d, c):
            j = lax.rem(me - d + sources, sources)
            pltpu.make_async_remote_copy(
                src_ref=buf.at[pi, padded(j)],
                dst_ref=buf.at[pi, padded(j)],
                send_sem=ss.at[j],
                recv_sem=rs.at[j],
                device_id={"expert": j // subs, "sub": j % subs},
                device_id_type=MESH,
            ).wait_recv()
            forward(j, pi, buf, fss, frs).start()
            return c

        lax.fori_loop(1, sources, pass_on, 0)
        compact(pi, buf, comp, moves)

        def take_pass(j, c):
            forward(j, other, buf, fss, frs).wait_recv()
            return c

        lax.fori_loop(0, sources, take_pass, 0)
        compact(other, buf, comp, moves)

    def gate_up(at, out, to):
        x = compx[pl.ds(at, BLOCK), :]
        out[pl.ds(to, BLOCK), 0:ff] = dot(x, gate[...]).astype(out.dtype)
        out[pl.ds(to, BLOCK), ff : 2 * ff] = dot(x, up[...]).astype(out.dtype)

    def grad(at, out, to):
        z = compz[pl.ds(at, BLOCK), 0:dh]
        out[pl.ds(to, BLOCK), :] = dot(z, down[...], NT).astype(out.dtype)

    def share_copy(d, src, buf, ss, rs, came):
        s = lax.rem(si + d, subs)
        at = s if came else si
        return pltpu.make_async_remote_copy(
            src_ref=buf.at[at] if came else src.at[pl.ds(pl.multiple_of(s * chunk, PAD), chunk)],
            dst_ref=buf.at[at],
            send_sem=ss.at[s],
            recv_sem=rs.at[at],
            device_id={"sub": s},
            device_id_type=MESH,
        )

    def exchange(work, src, own, buf, ss, rs):
        for d in range(1, subs):
            base = lax.rem(si + d, subs) * chunk

            def send_block(b, c):
                at = pl.multiple_of(base + b * BLOCK, PAD)
                work(at, src, at)
                return c

            lax.fori_loop(0, chunk // BLOCK, send_block, 0)
            share_copy(d, src, buf, ss, rs, False).start()

        def own_block(b, c):
            at = pl.multiple_of(si * chunk + b * BLOCK, PAD)
            work(at, own, pl.multiple_of(b * BLOCK, PAD))
            return c

        lax.fori_loop(0, chunk // BLOCK, own_block, 0)

    def summed(own, buf, to, k):
        v = own[pl.ds(to, BLOCK), k * ff : (k + 1) * ff]
        for d in range(1, subs):
            s = lax.rem(si + d, subs)
            v = v + buf[s, pl.ds(to, BLOCK), k * ff : (k + 1) * ff].astype(F32)
        return v

    take_rows(bufx, compx, x_send, x_recv, fx_send, fx_recv)
    loads[3].wait()
    loads[4].wait()
    exchange(gate_up, gu_send, gu_own, gu_buf, gu_ss, gu_rs)
    take_rows(bufz, compz, z_send, z_recv, fz_send, fz_recv)
    loads[5].wait()
    exchange(grad, hg_send, hg_own, hg_buf, hg_ss, hg_rs)

    hp_me = si * 2 + pi
    for d in range(1, subs):
        share_copy(d, gu_send, gu_buf, gu_ss, gu_rs, True).wait_recv()

    def hidden_block(b, c):
        to = pl.multiple_of(b * BLOCK, PAD)
        g, u = summed(gu_own, gu_buf, to, 0), summed(gu_own, gu_buf, to, 1)
        gu_own[pl.ds(to, BLOCK), 0:ff] = g
        gu_own[pl.ds(to, BLOCK), ff : 2 * ff] = u
        hidden = (g * (1.0 / (1.0 + jnp.exp(-g))) * u).astype(BF16)
        v = dot(hidden, ph[...], NT)
        hp_buf[hp_me, pl.ds(to, BLOCK), :] = jnp.concatenate(
            [v, jnp.zeros((BLOCK, LANES - rank_size), F32)], axis=1
        )
        return c

    lax.fori_loop(0, chunk // BLOCK, hidden_block, 0)

    def h_copy(d, came):
        q = lax.rem(hp_me + d, 2 * subs)
        at = q if came else hp_me
        return pltpu.make_async_remote_copy(
            src_ref=hp_buf.at[at],
            dst_ref=hp_buf.at[at],
            send_sem=h_ss.at[q],
            recv_sem=h_rs.at[at],
            device_id={"sub": q // 2, "pair": q % 2},
            device_id_type=MESH,
        )

    for d in range(1, 2 * subs):
        h_copy(d, False).start()
    for d in range(1, subs):
        share_copy(d, hg_send, hg_buf, hg_ss, hg_rs, True).wait_recv()

    def act_block(b, c):
        to = pl.multiple_of(b * BLOCK, PAD)
        g, u = gu_own[pl.ds(to, BLOCK), 0:ff], gu_own[pl.ds(to, BLOCK), ff : 2 * ff]
        h = summed(hg_own, hg_buf, to, 0)
        sig = 1.0 / (1.0 + jnp.exp(-g))
        at = pl.multiple_of(si * chunk + b * BLOCK, PAD)
        gbuf[pl.ds(at, BLOCK), 0:ff] = (h * u * sig * (1.0 + g * (1.0 - sig))).astype(BF16)
        gbuf[pl.ds(at, BLOCK), ff : 2 * ff] = (h * (g * sig)).astype(BF16)
        return c

    lax.fori_loop(0, chunk // BLOCK, act_block, 0)

    def g_copy(d, came):
        s = lax.rem(si + d, subs)
        at = s if came else si
        span = gbuf.at[pl.ds(pl.multiple_of(at * chunk, PAD), chunk)]
        return pltpu.make_async_remote_copy(
            src_ref=span,
            dst_ref=span,
            send_sem=g_ss.at[s],
            recv_sem=g_rs.at[at],
            device_id={"sub": s},
            device_id_type=MESH,
        )

    for d in range(1, subs):
        g_copy(d, False).start()

    rp, ret_send = compx, bufx.at[other]

    def swap(s):
        span = pl.ds(pl.multiple_of(s * chunk, PAD), chunk)
        return pltpu.make_async_remote_copy(
            src_ref=rp.at[span],
            dst_ref=rp_in.at[pl.ds(pl.multiple_of(s % (subs // 2) * chunk, PAD), chunk)],
            send_sem=p_ss.at[s],
            recv_sem=p_rs.at[s],
            device_id={"pair": other},
            device_id_type=MESH,
        )

    def back(j, came):
        at_e = j // subs if came else ei
        at_s = j % subs if came else si
        return pltpu.make_async_remote_copy(
            src_ref=ret_send.at[padded(j)],
            dst_ref=ret_buf.at[padded(at_e), pl.ds(pl.multiple_of(at_s * wx, LANES), wx)],
            send_sem=r_ss.at[j],
            recv_sem=r_rs.at[j if came else me],
            device_id={"expert": j // subs, "sub": j % subs},
            device_id_type=MESH,
        )

    per_chunk = chunk // CAP

    def route_chunk(s):
        def body(b, c):
            at = pl.multiple_of(s * chunk + b * BLOCK, PAD)
            v = dot(gbuf[pl.ds(at, BLOCK), 0:ff], gate[...], NT)
            v = v + dot(gbuf[pl.ds(at, BLOCK), ff : 2 * ff], up[...], NT)
            rp[pl.ds(at, BLOCK), :] = v.astype(BF16)
            return c

        lax.fori_loop(0, chunk // BLOCK, body, 0)
        first = s * per_chunk - pi * sources

        @pl.when(s * 2 // subs == other)
        def _():
            swap(s).start()

        @pl.when(s * 2 // subs == pi)
        def _():
            swap(s).wait_recv()

            def sum_block(b, c):
                at = pl.multiple_of(s * chunk + b * BLOCK, PAD)
                came = pl.multiple_of(s % (subs // 2) * chunk + b * BLOCK, PAD)
                v = rp[pl.ds(at, BLOCK), :].astype(F32) + rp_in[pl.ds(came, BLOCK), :].astype(F32)
                put = pl.multiple_of((first + b * GROUP) * PAD, GROUP * PAD)
                v = v.astype(BF16)
                keep = wx // LANES
                for k in range(keep):
                    w = dot(squeeze, v[:, tile(k)], TN)
                    for at_k, t, m in unfolders(dh // LANES):
                        if at_k == k:
                            w = w + dot(m, v[:, tile(t)], TN)
                    ret_send[pl.ds(put, GROUP * PAD), tile(k)] = w.astype(BF16)
                return c

            lax.fori_loop(0, chunk // BLOCK, sum_block, 0)

            def start_back(i, c):
                j = first + lax.rem(me + 1 + i, per_chunk)

                @pl.when(j != me)
                def _():
                    back(j, False).start()

                @pl.when(j == me)
                def _():
                    ret_buf[padded(ei), pl.ds(pl.multiple_of(si * wx, LANES), wx)] = ret_send[
                        padded(me), :
                    ]

                return c

            lax.fori_loop(0, per_chunk, start_back, 0)

    route_chunk(si)

    for d in range(1, 2 * subs):
        h_copy(d, True).wait_recv()
    share = rank_size // (2 * subs)
    spread_cols = gs.shape[0]
    row = lax.broadcasted_iota(jnp.int32, (LANES, spread_cols), 0)
    col = lax.broadcasted_iota(jnp.int32, (LANES, spread_cols), 1)
    repeat = jnp.where(row == hp_me * share + col % share, 1.0, 0.0).astype(BF16)
    want = (
        lax.broadcasted_iota(jnp.int32, (BLOCK, spread_cols), 1) // share + 1
    ).astype(F32)

    def example_block(b, acc):
        at = pl.multiple_of(b * BLOCK, PAD)
        ex = compz[pl.ds(at, BLOCK), dh:zw]
        code = ex[:, rank_size : rank_size + 1].astype(F32)
        spread = jnp.where(code == want, dot(ex, repeat), 0.0).astype(BF16)
        s = b // (chunk // BLOCK)
        to = pl.multiple_of((b % (chunk // BLOCK)) * BLOCK, PAD)
        hp = hp_buf[2 * s, pl.ds(to, BLOCK), :] + hp_buf[2 * s + 1, pl.ds(to, BLOCK), :]
        hi = hp.astype(BF16)
        rest = hp - hi.astype(F32)
        mid = rest.astype(BF16)
        low = (rest - mid.astype(F32)).astype(BF16)
        return acc + dot(spread, hi, TN) + dot(spread, mid, TN) + dot(spread, low, TN)

    gs[...] = lax.fori_loop(
        0, rows // BLOCK, example_block, jnp.zeros((spread_cols, LANES), F32)
    ).astype(BF16)
    piece = spread_cols // owners

    def e_copy(e, came):
        return pltpu.make_async_remote_copy(
            src_ref=gs.at[pl.ds(pl.multiple_of(e * piece, PAD), piece)],
            dst_ref=eg_buf.at[e if came else ei],
            send_sem=e_ss.at[e],
            recv_sem=e_rs.at[e if came else ei],
            device_id={"expert": e},
            device_id_type=MESH,
        )

    def start_e(d, c):
        e_copy(lax.rem(ei + d, owners), False).start()
        return c

    lax.fori_loop(1, owners, start_e, 0)
    eg_buf[ei] = gs[pl.ds(pl.multiple_of(ei * piece, PAD), piece), :]

    for d in range(1, subs):
        g_copy(d, True).wait_recv()
        route_chunk(lax.rem(si + d, subs))

    def take_e(d, c):
        e_copy(lax.rem(ei + d, owners), True).wait_recv()
        return c

    lax.fori_loop(1, owners, take_e, 0)
    eg = eg_buf[...].astype(F32)
    for x in range(4):
        eg_out[x] = eg[:, x * share : (x + 1) * share, 0:rank_size]

    def sent(d, c):
        j = lax.rem(me + d, sources)
        rows_to(d, px, bufx, x_send, x_recv).wait_send()
        rows_to(d, pz, bufz, z_send, z_recv).wait_send()
        back(j, False).wait_send()
        return c

    lax.fori_loop(1, sources, sent, 0)

    def sent_pass(j, c):
        forward(j, pi, bufx, fx_send, fx_recv).wait_send()
        forward(j, pi, bufz, fz_send, fz_recv).wait_send()
        return c

    lax.fori_loop(0, sources, sent_pass, 0)
    for d in range(1, subs):
        share_copy(d, gu_send, gu_buf, gu_ss, gu_rs, False).wait_send()
        share_copy(d, hg_send, hg_buf, hg_ss, hg_rs, False).wait_send()
        g_copy(d, False).wait_send()
    for d in range(1, 2 * subs):
        h_copy(d, False).wait_send()
    for i in range(subs // 2):
        swap(other * (subs // 2) + i).wait_send()

    def sent_e(d, c):
        e_copy(lax.rem(ei + d, owners), False).wait_send()
        return c

    lax.fori_loop(1, owners, sent_e, 0)

    def take_back(d, c):
        back(lax.rem(me + d, sources), True).wait_recv()
        return c

    lax.fori_loop(1, sources, take_back, 0)
    keep, segs = segments(dh // LANES)
    slots = ret_buf.shape[0]
    moves = [
        (k, t, mover(slots, PAD, slots, PAD, lo - shift, hi - shift, -shift))
        for k, t, lo, hi, shift in segs
    ]
    for s in range(subs):
        ret_out[:, s * dh : s * dh + wx] = ret_buf[:, s * wx : (s + 1) * wx]
        for to in range(keep, dh // LANES):
            v = sum(
                dot(m, ret_buf[:, s * wx + k * LANES : s * wx + (k + 1) * LANES])
                for k, t, m in moves
                if t == to
            )
            ret_out[:, s * dh + to * LANES : s * dh + (to + 1) * LANES] = v.astype(BF16)


def per_device(
    tokens, out_grad, routes, route_weight, example_id, gate_w, up_w, down_w, proj_grad, proj_hidden
):
    owners = lax.axis_size("expert")
    subs = lax.axis_size("sub")
    local_tokens, width = tokens.shape
    rank_size = proj_grad.shape[0]
    slots = owners * PAD
    dh = width // subs
    zw = dh + LANES
    wx, wz = segments(dh // LANES)[0] * LANES, segments(zw // LANES)[0] * LANES
    ff = gate_w.shape[2]
    sources = owners * subs
    rows = sources * 2 * CAP
    chunk = rows // subs
    examples = 4 * owners
    share = rank_size // (2 * subs)
    piece = 4 * share
    vmem = pl.BlockSpec(memory_space=pltpu.VMEM)
    hbm = pl.BlockSpec(memory_space=pl.ANY)
    dma = pltpu.SemaphoreType.DMA

    def space(*shape, kind=BF16):
        return pltpu.VMEM(shape, kind)

    returned, pick_token, example_grads = pl.pallas_call(
        functools.partial(kernel, owners, subs, rank_size),
        out_shape=(
            jax.ShapeDtypeStruct((slots, width), BF16),
            jax.ShapeDtypeStruct((slots, local_tokens), BF16),
            jax.ShapeDtypeStruct((4, owners, share, rank_size), F32),
        ),
        in_specs=[vmem] * 3 + [hbm] * 6 + [vmem],
        out_specs=(vmem, vmem, vmem),
        scratch_shapes=[
            space(local_tokens, width),
            space(local_tokens, width),
            space(dh, ff),
            space(dh, ff),
            space(ff, dh),
            space(rank_size, width),
            space(slots, subs * wx),
            space(slots, subs * wz),
            space(2, sources * PAD, wx),
            space(2, sources * PAD, wz),
            space(rows, dh),
            space(rows, zw),
            space(rows, 2 * ff),
            space(chunk, 2 * ff, kind=F32),
            space(subs, chunk, 2 * ff),
            space(rows, ff),
            space(chunk, ff, kind=F32),
            space(subs, chunk, ff),
            space(rows, 2 * ff),
            space(2 * subs, chunk, LANES, kind=F32),
            space(rows // 2, dh),
            space(slots, subs * wx),
            space(examples * share, LANES),
            space(owners, piece, LANES),
            dma((6,)),
        ]
        + [dma((sources,))] * 8
        + [dma((subs,))] * 6
        + [dma((2 * subs,))] * 2
        + [dma((subs,))] * 2
        + [dma((sources,))] * 2
        + [dma((owners,))] * 2,
        compiler_params=pltpu.CompilerParams(
            collective_id=0, has_side_effects=True, vmem_limit_bytes=60 * 1024 * 1024
        ),
    )(
        routes.T, route_weight.T, example_id[None, :], tokens, out_grad,
        gate_w[0], up_w[0], down_w[0], proj_grad, proj_hidden,
    )
    input_grad = dot(pick_token, returned, TN).astype(BF16)
    return (input_grad, example_grads)


def solution(mesh):
    return jax.shard_map(
        per_device,
        mesh=mesh,
        in_specs=(
            P(("groups", "expert", "sub", "pair"), None),
            P(("groups", "expert", "sub", "pair"), None),
            P(("groups", "expert", "sub", "pair"), None),
            P(("groups", "expert", "sub", "pair"), None),
            P(("groups", "expert", "sub", "pair")),
            P("expert", "sub", "pair"),
            P("expert", "sub", "pair"),
            P("expert", "pair", "sub"),
            P(),
            P(None, "pair"),
        ),
        out_specs=(
            P(("groups", "expert", "sub", "pair"), None),
            P(("groups", "expert"), None, ("sub", "pair"), None),
        ),
        check_vma=False,
    )
```

```python
import functools

import jax
import jax.numpy as jnp
from jax import lax
from jax.experimental import pallas as pl
from jax.experimental.pallas import tpu as pltpu
from jax.sharding import PartitionSpec as P

CAP = 10
PAD = 16
GROUP = 8
BLOCK = CAP * GROUP
LANES = 128
MESH = pl.DeviceIdType.MESH
F32 = jnp.float32
BF16 = jnp.bfloat16
NT = (((1,), (1,)), ((), ()))
TN = (((0,), (0,)), ((), ()))


def dot(a, b, dims=(((1,), (0,)), ((), ()))):
    return lax.dot_general(a, b, dims, preferred_element_type=F32)


def pack_matrix(rows, cols):
    i = lax.broadcasted_iota(jnp.int32, (rows, cols), 0)
    k = lax.broadcasted_iota(jnp.int32, (rows, cols), 1)
    hit = (k // PAD == i // CAP) & (k % PAD == i % CAP)
    return jnp.where(hit, 1.0, 0.0).astype(BF16)


def segments(tiles):
    keep = -(-tiles * CAP // PAD)
    found = {}
    for f in range(CAP * (tiles - keep)):
        k, i = divmod(f, PAD - CAP)
        key = (k, keep + f // CAP)
        lo, _, shift = found.get(key, (CAP + i, 0, CAP + i - f % CAP))
        found[key] = (lo, CAP + i + 1, shift)
    return keep, [(k, t) + v for (k, t), v in found.items()]


def tile(k, n=1):
    return slice(k * LANES, (k + n) * LANES)


def mover(to_rows, to_step, from_rows, from_step, lo, hi, shift):
    a = lax.broadcasted_iota(jnp.int32, (to_rows, from_rows), 0)
    b = lax.broadcasted_iota(jnp.int32, (to_rows, from_rows), 1)
    within = a % to_step
    hit = (a // to_step == b // from_step) & (within - b % from_step == shift)
    return jnp.where(hit & (within >= lo) & (within < hi), 1.0, 0.0).astype(BF16)


def fold(value):
    keep, segs = segments(value.shape[1] // LANES)
    n = value.shape[0]
    parts = [value[:, tile(k)].astype(F32) for k in range(keep)]
    for k, t, lo, hi, shift in segs:
        parts[k] = parts[k] + dot(mover(n, PAD, n, PAD, lo, hi, shift), value[:, tile(t)])
    return jnp.concatenate([p.astype(BF16) for p in parts], axis=1)


def kernel(
    owners, subs, rank_size,
    routes_t, weight_t, example, tokens, out_grad, gate_in, up_in, down_in, proj, ph,
    ret_out, pick_out, eg_out,
    tok, og, gate, up, down, pj, px, pz, bufx, bufz, compx, compz,
    gu_send, gu_own, gu_buf, hg_send, hg_own, hg_buf, gbuf, hp_buf, rp_in, ret_buf,
    gs, eg_buf,
    load_sem, x_send, x_recv, z_send, z_recv, fx_send, fx_recv, fz_send, fz_recv,
    gu_ss, gu_rs, hg_ss, hg_rs, g_ss, g_rs, h_ss, h_rs, p_ss, p_rs, r_ss, r_rs, e_ss, e_rs,
):
    ei, si, pi = lax.axis_index("expert"), lax.axis_index("sub"), lax.axis_index("pair")
    other = 1 - pi
    sources = owners * subs
    me = ei * subs + si
    rows = compx.shape[0]
    half = rows // 2
    chunk = rows // subs
    dh = compx.shape[1]
    zw = compz.shape[1]
    wx, wz = bufx.shape[2], bufz.shape[2]
    ff = gate.shape[1]

    loads = [
        pltpu.make_async_copy(a, b, load_sem.at[k])
        for k, (a, b) in enumerate(
            [(tokens, tok), (out_grad, og), (proj, pj), (gate_in, gate), (up_in, up), (down_in, down)]
        )
    ]
    for load in loads:
        load.start()

    barrier = pltpu.get_barrier_semaphore()

    def greet(d, c):
        j = lax.rem(me + d, sources)
        pl.semaphore_signal(
            barrier, 1, device_id={"expert": j // subs, "sub": j % subs}, device_id_type=MESH
        )
        return c

    lax.fori_loop(1, sources, greet, 0)
    for d in range(subs):
        pl.semaphore_signal(
            barrier, 1, device_id={"sub": lax.rem(si + d, subs), "pair": other}, device_id_type=MESH
        )

    tokens_here = tok.shape[0]
    named = [(routes_t[...] == e) for e in range(owners)]
    taken = jnp.concatenate(
        [jnp.sum(jnp.where(n, 1.0, 0.0), axis=0, keepdims=True) for n in named], axis=0
    )
    weights = weight_t[...].astype(F32)
    chosen = [jnp.sum(jnp.where(n, weights, 0.0), axis=0, keepdims=True) for n in named]
    lower = lax.broadcasted_iota(jnp.int32, (tokens_here, tokens_here), 0)
    upper = lax.broadcasted_iota(jnp.int32, (tokens_here, tokens_here), 1)
    before = dot(taken.astype(BF16), jnp.where(lower < upper, 1.0, 0.0).astype(BF16))
    slot = lax.broadcasted_iota(jnp.int32, (PAD, tokens_here), 0).astype(F32)
    hits, slot_weights, slot_codes = [], [], []
    codes = (example[...] + 1).astype(F32)
    for e in range(owners):
        hit = jnp.where((before[e : e + 1] == slot) & (taken[e : e + 1] > 0.5), 1.0, 0.0)
        hits.append(hit)
        slot_weights.append(jnp.sum(hit * chosen[e], axis=1, keepdims=True))
        slot_codes.append(jnp.sum(hit * codes, axis=1, keepdims=True))
    pick = jnp.concatenate(hits, axis=0).astype(BF16)
    slot_weight = jnp.concatenate(slot_weights, axis=0)
    slot_code = jnp.concatenate(slot_codes, axis=0)
    pick_out[...] = pick
    loads[0].wait()
    picked = dot(pick, tok[...]).astype(BF16)
    for s in range(subs):
        px[:, s * wx : (s + 1) * wx] = fold(picked[:, s * dh : (s + 1) * dh])
    pl.semaphore_wait(barrier, sources - 1 + subs)

    def padded(j):
        return pl.ds(pl.multiple_of(j * PAD, PAD), PAD)

    def rows_to(d, pack, buf, ss, rs):
        j = lax.rem(me + d, sources)
        e, s = j // subs, j % subs
        wide = buf.shape[2]
        return pltpu.make_async_remote_copy(
            src_ref=pack.at[padded(e), pl.ds(pl.multiple_of(s * wide, LANES), wide)],
            dst_ref=buf.at[pi, padded(me)],
            send_sem=ss.at[j],
            recv_sem=rs.at[me],
            device_id={"expert": e, "sub": s},
            device_id_type=MESH,
        )

    def forward(j, half_at, buf, ss, rs):
        return pltpu.make_async_remote_copy(
            src_ref=buf.at[half_at, padded(j)],
            dst_ref=buf.at[half_at, padded(j)],
            send_sem=ss.at[j],
            recv_sem=rs.at[j],
            device_id={"pair": other},
            device_id_type=MESH,
        )

    def send_rows(pack, buf, ss, rs, fss, frs):
        def body(d, c):
            rows_to(d, pack, buf, ss, rs).start()
            return c

        lax.fori_loop(1, sources, body, 0)
        wide = buf.shape[2]
        buf[pi, padded(me), :] = pack[padded(ei), pl.ds(pl.multiple_of(si * wide, LANES), wide)]
        forward(me, pi, buf, fss, frs).start()

    send_rows(px, bufx, x_send, x_recv, fx_send, fx_recv)

    loads[1].wait()
    scaled = (slot_weight * dot(pick, og[...])).astype(BF16)
    loads[2].wait()
    projected = dot(scaled, pj[...], NT).astype(BF16)
    lane = lax.broadcasted_iota(jnp.int32, (owners * PAD, LANES - rank_size), 1)
    extra = jnp.concatenate(
        [projected, jnp.where(lane == 0, slot_code, 0.0).astype(BF16)], axis=1
    )
    for s in range(subs):
        pz[:, s * wz : (s + 1) * wz] = fold(
            jnp.concatenate([scaled[:, s * dh : (s + 1) * dh], extra], axis=1)
        )
    send_rows(pz, bufz, z_send, z_recv, fz_send, fz_recv)

    squeeze = pack_matrix(BLOCK, GROUP * PAD)

    def unfolders(tiles):
        return [
            (k, t, mover(BLOCK, CAP, GROUP * PAD, PAD, lo - shift, hi - shift, -shift))
            for k, t, lo, hi, shift in segments(tiles)[1]
        ]

    def compact(half_at, buf, comp, moves):
        keep = buf.shape[2] // LANES

        def body(g, c):
            part = buf[half_at, pl.ds(pl.multiple_of(g * GROUP * PAD, GROUP * PAD), GROUP * PAD), :]
            at = pl.multiple_of(half_at * half + g * BLOCK, PAD)
            comp[pl.ds(at, BLOCK), tile(0, keep)] = dot(squeeze, part).astype(BF16)
            for t in range(keep, comp.shape[1] // LANES):
                v = sum(dot(m, part[:, tile(k)]) for k, to, m in moves if to == t)
                comp[pl.ds(at, BLOCK), tile(t)] = v.astype(BF16)
            return c

        lax.fori_loop(0, sources // GROUP, body, 0)

    def take_rows(buf, comp, ss, rs, fss, frs):
        moves = unfolders(comp.shape[1] // LANES)

        def pass_on(d, c):
            j = lax.rem(me - d + sources, sources)
            pltpu.make_async_remote_copy(
                src_ref=buf.at[pi, padded(j)],
                dst_ref=buf.at[pi, padded(j)],
                send_sem=ss.at[j],
                recv_sem=rs.at[j],
                device_id={"expert": j // subs, "sub": j % subs},
                device_id_type=MESH,
            ).wait_recv()
            forward(j, pi, buf, fss, frs).start()
            return c

        lax.fori_loop(1, sources, pass_on, 0)
        compact(pi, buf, comp, moves)

        def take_pass(j, c):
            forward(j, other, buf, fss, frs).wait_recv()
            return c

        lax.fori_loop(0, sources, take_pass, 0)
        compact(other, buf, comp, moves)

    def gate_up(at, out, to):
        x = compx[pl.ds(at, BLOCK), :]
        out[pl.ds(to, BLOCK), 0:ff] = dot(x, gate[...]).astype(out.dtype)
        out[pl.ds(to, BLOCK), ff : 2 * ff] = dot(x, up[...]).astype(out.dtype)

    def grad(at, out, to):
        z = compz[pl.ds(at, BLOCK), 0:dh]
        out[pl.ds(to, BLOCK), :] = dot(z, down[...], NT).astype(out.dtype)

    def share_copy(d, src, buf, ss, rs, came):
        s = lax.rem(si + d, subs)
        at = s if came else si
        return pltpu.make_async_remote_copy(
            src_ref=buf.at[at] if came else src.at[pl.ds(pl.multiple_of(s * chunk, PAD), chunk)],
            dst_ref=buf.at[at],
            send_sem=ss.at[s],
            recv_sem=rs.at[at],
            device_id={"sub": s},
            device_id_type=MESH,
        )

    def exchange(work, src, own, buf, ss, rs):
        for d in range(1, subs):
            base = lax.rem(si + d, subs) * chunk

            def send_block(b, c):
                at = pl.multiple_of(base + b * BLOCK, PAD)
                work(at, src, at)
                return c

            lax.fori_loop(0, chunk // BLOCK, send_block, 0)
            share_copy(d, src, buf, ss, rs, False).start()

        def own_block(b, c):
            at = pl.multiple_of(si * chunk + b * BLOCK, PAD)
            work(at, own, pl.multiple_of(b * BLOCK, PAD))
            return c

        lax.fori_loop(0, chunk // BLOCK, own_block, 0)

    def summed(own, buf, to, k):
        v = own[pl.ds(to, BLOCK), k * ff : (k + 1) * ff]
        for d in range(1, subs):
            s = lax.rem(si + d, subs)
            v = v + buf[s, pl.ds(to, BLOCK), k * ff : (k + 1) * ff].astype(F32)
        return v

    take_rows(bufx, compx, x_send, x_recv, fx_send, fx_recv)
    loads[3].wait()
    loads[4].wait()
    exchange(gate_up, gu_send, gu_own, gu_buf, gu_ss, gu_rs)
    take_rows(bufz, compz, z_send, z_recv, fz_send, fz_recv)
    loads[5].wait()
    exchange(grad, hg_send, hg_own, hg_buf, hg_ss, hg_rs)

    hp_me = si * 2 + pi
    for d in range(1, subs):
        share_copy(d, gu_send, gu_buf, gu_ss, gu_rs, True).wait_recv()

    def hidden_block(b, c):
        to = pl.multiple_of(b * BLOCK, PAD)
        g, u = summed(gu_own, gu_buf, to, 0), summed(gu_own, gu_buf, to, 1)
        gu_own[pl.ds(to, BLOCK), 0:ff] = g
        gu_own[pl.ds(to, BLOCK), ff : 2 * ff] = u
        hidden = (g * (1.0 / (1.0 + jnp.exp(-g))) * u).astype(BF16)
        v = dot(hidden, ph[...], NT)
        hp_buf[hp_me, pl.ds(to, BLOCK), :] = jnp.concatenate(
            [v, jnp.zeros((BLOCK, LANES - rank_size), F32)], axis=1
        )
        return c

    lax.fori_loop(0, chunk // BLOCK, hidden_block, 0)

    def h_copy(d, came):
        q = lax.rem(hp_me + d, 2 * subs)
        at = q if came else hp_me
        return pltpu.make_async_remote_copy(
            src_ref=hp_buf.at[at],
            dst_ref=hp_buf.at[at],
            send_sem=h_ss.at[q],
            recv_sem=h_rs.at[at],
            device_id={"sub": q // 2, "pair": q % 2},
            device_id_type=MESH,
        )

    for d in range(1, 2 * subs):
        h_copy(d, False).start()
    for d in range(1, subs):
        share_copy(d, hg_send, hg_buf, hg_ss, hg_rs, True).wait_recv()

    def act_block(b, c):
        to = pl.multiple_of(b * BLOCK, PAD)
        g, u = gu_own[pl.ds(to, BLOCK), 0:ff], gu_own[pl.ds(to, BLOCK), ff : 2 * ff]
        h = summed(hg_own, hg_buf, to, 0)
        sig = 1.0 / (1.0 + jnp.exp(-g))
        at = pl.multiple_of(si * chunk + b * BLOCK, PAD)
        gbuf[pl.ds(at, BLOCK), 0:ff] = (h * u * sig * (1.0 + g * (1.0 - sig))).astype(BF16)
        gbuf[pl.ds(at, BLOCK), ff : 2 * ff] = (h * (g * sig)).astype(BF16)
        return c

    lax.fori_loop(0, chunk // BLOCK, act_block, 0)

    def g_copy(d, came):
        s = lax.rem(si + d, subs)
        at = s if came else si
        span = gbuf.at[pl.ds(pl.multiple_of(at * chunk, PAD), chunk)]
        return pltpu.make_async_remote_copy(
            src_ref=span,
            dst_ref=span,
            send_sem=g_ss.at[s],
            recv_sem=g_rs.at[at],
            device_id={"sub": s},
            device_id_type=MESH,
        )

    for d in range(1, subs):
        g_copy(d, False).start()

    rp, ret_send = compx, bufx.at[other]

    def swap(s):
        span = pl.ds(pl.multiple_of(s * chunk, PAD), chunk)
        return pltpu.make_async_remote_copy(
            src_ref=rp.at[span],
            dst_ref=rp_in.at[pl.ds(pl.multiple_of(s % (subs // 2) * chunk, PAD), chunk)],
            send_sem=p_ss.at[s],
            recv_sem=p_rs.at[s],
            device_id={"pair": other},
            device_id_type=MESH,
        )

    def back(j, came):
        at_e = j // subs if came else ei
        at_s = j % subs if came else si
        return pltpu.make_async_remote_copy(
            src_ref=ret_send.at[padded(j)],
            dst_ref=ret_buf.at[padded(at_e), pl.ds(pl.multiple_of(at_s * wx, LANES), wx)],
            send_sem=r_ss.at[j],
            recv_sem=r_rs.at[j if came else me],
            device_id={"expert": j // subs, "sub": j % subs},
            device_id_type=MESH,
        )

    per_chunk = chunk // CAP

    def route_chunk(s):
        def body(b, c):
            at = pl.multiple_of(s * chunk + b * BLOCK, PAD)
            v = dot(gbuf[pl.ds(at, BLOCK), 0:ff], gate[...], NT)
            v = v + dot(gbuf[pl.ds(at, BLOCK), ff : 2 * ff], up[...], NT)
            rp[pl.ds(at, BLOCK), :] = v.astype(BF16)
            return c

        lax.fori_loop(0, chunk // BLOCK, body, 0)
        first = s * per_chunk - pi * sources

        @pl.when(s * 2 // subs == other)
        def _():
            swap(s).start()

        @pl.when(s * 2 // subs == pi)
        def _():
            swap(s).wait_recv()

            def sum_block(b, c):
                at = pl.multiple_of(s * chunk + b * BLOCK, PAD)
                came = pl.multiple_of(s % (subs // 2) * chunk + b * BLOCK, PAD)
                v = rp[pl.ds(at, BLOCK), :].astype(F32) + rp_in[pl.ds(came, BLOCK), :].astype(F32)
                put = pl.multiple_of((first + b * GROUP) * PAD, GROUP * PAD)
                v = v.astype(BF16)
                keep = wx // LANES
                for k in range(keep):
                    w = dot(squeeze, v[:, tile(k)], TN)
                    for at_k, t, m in unfolders(dh // LANES):
                        if at_k == k:
                            w = w + dot(m, v[:, tile(t)], TN)
                    ret_send[pl.ds(put, GROUP * PAD), tile(k)] = w.astype(BF16)
                return c

            lax.fori_loop(0, chunk // BLOCK, sum_block, 0)

            def start_back(i, c):
                j = first + lax.rem(me + 1 + i, per_chunk)

                @pl.when(j != me)
                def _():
                    back(j, False).start()

                @pl.when(j == me)
                def _():
                    ret_buf[padded(ei), pl.ds(pl.multiple_of(si * wx, LANES), wx)] = ret_send[
                        padded(me), :
                    ]

                return c

            lax.fori_loop(0, per_chunk, start_back, 0)

    route_chunk(si)

    for d in range(1, 2 * subs):
        h_copy(d, True).wait_recv()
    share = rank_size // (2 * subs)
    spread_cols = gs.shape[0]
    row = lax.broadcasted_iota(jnp.int32, (LANES, spread_cols), 0)
    col = lax.broadcasted_iota(jnp.int32, (LANES, spread_cols), 1)
    repeat = jnp.where(row == hp_me * share + col % share, 1.0, 0.0).astype(BF16)
    want = (
        lax.broadcasted_iota(jnp.int32, (BLOCK, spread_cols), 1) // share + 1
    ).astype(F32)

    def example_block(b, acc):
        at = pl.multiple_of(b * BLOCK, PAD)
        ex = compz[pl.ds(at, BLOCK), dh:zw]
        code = ex[:, rank_size : rank_size + 1].astype(F32)
        spread = jnp.where(code == want, dot(ex, repeat), 0.0).astype(BF16)
        s = b // (chunk // BLOCK)
        to = pl.multiple_of((b % (chunk // BLOCK)) * BLOCK, PAD)
        hp = hp_buf[2 * s, pl.ds(to, BLOCK), :] + hp_buf[2 * s + 1, pl.ds(to, BLOCK), :]
        hi = hp.astype(BF16)
        rest = hp - hi.astype(F32)
        mid = rest.astype(BF16)
        low = (rest - mid.astype(F32)).astype(BF16)
        return acc + dot(spread, hi, TN) + dot(spread, mid, TN) + dot(spread, low, TN)

    gs[...] = lax.fori_loop(
        0, rows // BLOCK, example_block, jnp.zeros((spread_cols, LANES), F32)
    ).astype(BF16)
    piece = spread_cols // owners

    def e_copy(e, came):
        return pltpu.make_async_remote_copy(
            src_ref=gs.at[pl.ds(pl.multiple_of(e * piece, PAD), piece)],
            dst_ref=eg_buf.at[e if came else ei],
            send_sem=e_ss.at[e],
            recv_sem=e_rs.at[e if came else ei],
            device_id={"expert": e},
            device_id_type=MESH,
        )

    def start_e(d, c):
        e_copy(lax.rem(ei + d, owners), False).start()
        return c

    lax.fori_loop(1, owners, start_e, 0)
    eg_buf[ei] = gs[pl.ds(pl.multiple_of(ei * piece, PAD), piece), :]

    for d in range(1, subs):
        g_copy(d, True).wait_recv()
        route_chunk(lax.rem(si + d, subs))

    def take_e(d, c):
        e_copy(lax.rem(ei + d, owners), True).wait_recv()
        return c

    lax.fori_loop(1, owners, take_e, 0)
    eg = eg_buf[...].astype(F32)
    for x in range(4):
        eg_out[x] = eg[:, x * share : (x + 1) * share, 0:rank_size]

    def sent(d, c):
        j = lax.rem(me + d, sources)
        rows_to(d, px, bufx, x_send, x_recv).wait_send()
        rows_to(d, pz, bufz, z_send, z_recv).wait_send()
        back(j, False).wait_send()
        return c

    lax.fori_loop(1, sources, sent, 0)

    def sent_pass(j, c):
        forward(j, pi, bufx, fx_send, fx_recv).wait_send()
        forward(j, pi, bufz, fz_send, fz_recv).wait_send()
        return c

    lax.fori_loop(0, sources, sent_pass, 0)
    for d in range(1, subs):
        share_copy(d, gu_send, gu_buf, gu_ss, gu_rs, False).wait_send()
        share_copy(d, hg_send, hg_buf, hg_ss, hg_rs, False).wait_send()
        g_copy(d, False).wait_send()
    for d in range(1, 2 * subs):
        h_copy(d, False).wait_send()
    for i in range(subs // 2):
        swap(other * (subs // 2) + i).wait_send()

    def sent_e(d, c):
        e_copy(lax.rem(ei + d, owners), False).wait_send()
        return c

    lax.fori_loop(1, owners, sent_e, 0)

    def take_back(d, c):
        back(lax.rem(me + d, sources), True).wait_recv()
        return c

    lax.fori_loop(1, sources, take_back, 0)
    keep, segs = segments(dh // LANES)
    slots = ret_buf.shape[0]
    moves = [
        (k, t, mover(slots, PAD, slots, PAD, lo - shift, hi - shift, -shift))
        for k, t, lo, hi, shift in segs
    ]
    for s in range(subs):
        ret_out[:, s * dh : s * dh + wx] = ret_buf[:, s * wx : (s + 1) * wx]
        for to in range(keep, dh // LANES):
            v = sum(
                dot(m, ret_buf[:, s * wx + k * LANES : s * wx + (k + 1) * LANES])
                for k, t, m in moves
                if t == to
            )
            ret_out[:, s * dh + to * LANES : s * dh + (to + 1) * LANES] = v.astype(BF16)


def spread_rows(pick, rows, out):
    out[...] = dot(pick[...], rows[...], TN).astype(BF16)


def per_device(
    tokens, out_grad, routes, route_weight, example_id, gate_w, up_w, down_w, proj_grad, proj_hidden
):
    owners = lax.axis_size("expert")
    subs = lax.axis_size("sub")
    local_tokens, width = tokens.shape
    rank_size = proj_grad.shape[0]
    slots = owners * PAD
    dh = width // subs
    zw = dh + LANES
    wx, wz = segments(dh // LANES)[0] * LANES, segments(zw // LANES)[0] * LANES
    ff = gate_w.shape[2]
    sources = owners * subs
    rows = sources * 2 * CAP
    chunk = rows // subs
    examples = 4 * owners
    share = rank_size // (2 * subs)
    piece = 4 * share
    vmem = pl.BlockSpec(memory_space=pltpu.VMEM)
    hbm = pl.BlockSpec(memory_space=pl.ANY)
    dma = pltpu.SemaphoreType.DMA

    def space(*shape, kind=BF16):
        return pltpu.VMEM(shape, kind)

    returned, pick_token, example_grads = pl.pallas_call(
        functools.partial(kernel, owners, subs, rank_size),
        out_shape=(
            jax.ShapeDtypeStruct((slots, width), BF16),
            jax.ShapeDtypeStruct((slots, local_tokens), BF16),
            jax.ShapeDtypeStruct((4, owners, share, rank_size), F32),
        ),
        in_specs=[vmem] * 3 + [hbm] * 6 + [vmem],
        out_specs=(vmem, vmem, vmem),
        scratch_shapes=[
            space(local_tokens, width),
            space(local_tokens, width),
            space(dh, ff),
            space(dh, ff),
            space(ff, dh),
            space(rank_size, width),
            space(slots, subs * wx),
            space(slots, subs * wz),
            space(2, sources * PAD, wx),
            space(2, sources * PAD, wz),
            space(rows, dh),
            space(rows, zw),
            space(rows, 2 * ff),
            space(chunk, 2 * ff, kind=F32),
            space(subs, chunk, 2 * ff),
            space(rows, ff),
            space(chunk, ff, kind=F32),
            space(subs, chunk, ff),
            space(rows, 2 * ff),
            space(2 * subs, chunk, LANES, kind=F32),
            space(rows // 2, dh),
            space(slots, subs * wx),
            space(examples * share, LANES),
            space(owners, piece, LANES),
            dma((6,)),
        ]
        + [dma((sources,))] * 8
        + [dma((subs,))] * 6
        + [dma((2 * subs,))] * 2
        + [dma((subs,))] * 2
        + [dma((sources,))] * 2
        + [dma((owners,))] * 2,
        compiler_params=pltpu.CompilerParams(
            collective_id=0, has_side_effects=True, vmem_limit_bytes=60 * 1024 * 1024
        ),
    )(
        routes.T, route_weight.T, example_id[None, :], tokens, out_grad,
        gate_w[0], up_w[0], down_w[0], proj_grad, proj_hidden,
    )
    input_grad = pl.pallas_call(
        spread_rows,
        out_shape=jax.ShapeDtypeStruct((local_tokens, width), BF16),
        in_specs=[vmem] * 2,
        out_specs=vmem,
    )(pick_token, returned)
    return (input_grad, example_grads)


def solution(mesh):
    return jax.shard_map(
        per_device,
        mesh=mesh,
        in_specs=(
            P(("groups", "expert", "sub", "pair"), None),
            P(("groups", "expert", "sub", "pair"), None),
            P(("groups", "expert", "sub", "pair"), None),
            P(("groups", "expert", "sub", "pair"), None),
            P(("groups", "expert", "sub", "pair")),
            P("expert", "sub", "pair"),
            P("expert", "sub", "pair"),
            P("expert", "pair", "sub"),
            P(),
            P(None, "pair"),
        ),
        out_specs=(
            P(("groups", "expert", "sub", "pair"), None),
            P(("groups", "expert"), None, ("sub", "pair"), None),
        ),
        check_vma=False,
    )
```
